256 devices in a mesh: row: 16 (over y_hi, z), col: 16 (over y_lo, x, core).
Axes of the slice: x: 4, y: 4 (y_hi: 2, y_lo: 2; y = y_hi * 2 + y_lo), z: 8, core: 2. Of those that a mesh axis runs over, the one named last changes fastest.
Arguments:
- start_rows: int32 [4], replicated, may hold values from 0 to 13, as said below
- initial: bfloat16 [4, 16, 256, 8, 256], P(None, 'col'), may hold values from -6 to 6
- site_tensors: bfloat16 [16, 16, 4096], P('row', 'col'), may hold values from -4 to 4
- charges: int32 [16, 16, 4, 8], P('row', 'col'), may hold values from 0 to 2
- right_proj: bfloat16 [16, 16, 256, 8, 256], P('row', 'col'), may hold values from -0.125 to 0.125
- left_proj: bfloat16 [16, 16, 256, 8, 256], P('row', 'col'), may hold values from -0.125 to 0.125
- kept_ranks: int32 [16, 16], P('row', 'col'), may hold values from 128 to 256
Outputs:
- absorbed: bfloat16 [16, 16, 256, 8, 256], P('row', 'col')
The draws below stay inside these ranges and needn't reach their ends.
Inputs may be any that keep to these rules, and one draw needn't show every extreme that they name: `start_rows`: the start rows are distinct; one is 0 and one is 13.
All inputs are finite; a program needn't handle non-finite values.
Results may differ from the reference program's by a relative error of at most 0.02.
Values may be sent and summed in bfloat16 or wider, within the bound.
A program may use at most 64 MiB of HBM per device.

```python
import jax
import jax.numpy as jnp
from jax import lax

CHI = 256
D = 8
ENVS = 4
ABSORB = 3
ROWS = 16
COLS = 16
N_ROW = 16


def draw_start_rows(key, part):
    key = jax.random.fold_in(key, 7)
    first_key, second_key = jax.random.split(key)
    middle = jax.random.permutation(first_key, N_ROW - 4)[:ENVS - 2] + 1
    values = jnp.concatenate([jnp.array([0, N_ROW - 3], jnp.int32), middle.astype(jnp.int32)])
    order = jax.random.permutation(second_key, ENVS)
    return values[order].astype(jnp.int32)


def touch_ends(values, key, low, top_value):
    place = [jax.random.randint(jax.random.fold_in(key, axis), (), 0, length) for axis, length in enumerate(values.shape)]
    main_axis = values.shape.index(max(values.shape))
    beside = place[:main_axis] + [(place[main_axis] + 1) % values.shape[main_axis]] + place[main_axis + 1:]
    return values.at[tuple(place)].set(low).at[tuple(beside)].set(top_value)


def steps_of(rng, extent, pieces, least, largest):
    def one(position, blocks):
        draws = jax.random.uniform(jax.random.fold_in(jax.random.fold_in(rng, 6), position), (blocks,), jnp.float32, least / len(pieces), largest / len(pieces))
        return jnp.repeat(jnp.exp(draws), extent[position] // blocks).reshape((-1,) + (1,) * (len(extent) - position - 1))

    loudness = one(*pieces[0])
    for cut in pieces[1:]:
        loudness = loudness * one(*cut)
    return loudness


def normal_values(rng, dims, deviation, limit, shards=(), held_as=jnp.bfloat16):
    entries = deviation * jax.random.normal(rng, dims, jnp.float32)
    if shards:
        entries = entries * steps_of(rng, dims, shards, -0.22, 0.18)
    return jnp.clip(entries, -limit, limit).astype(held_as)


def setup_inputs(seed: int = 0) -> dict:
    splits = jax.random.split(jax.random.key(seed), 8)
    start_rows = draw_start_rows(jax.random.fold_in(splits[7], 71), 0)
    initial = normal_values(splits[1], (ENVS, COLS, CHI, D, CHI), 1.0, 6.0, ((1, 16),))
    site_tensors = normal_values(splits[2], (ROWS, COLS, D * D * D * D), 0.8, 4.0, ((0, 16), (1, 16)))
    charges = touch_ends(jax.random.randint(splits[3], (ROWS, COLS, 4, D), 0, 3), jax.random.fold_in(splits[3], 1), 0, 2).astype(jnp.int32)
    right_proj = normal_values(splits[4], (ROWS, COLS, CHI, D, CHI), (CHI * D) ** -0.5, 0.125, ((0, 16), (1, 16)))
    left_proj = normal_values(splits[5], (ROWS, COLS, CHI, D, CHI), (CHI * D) ** -0.5, 0.125, ((0, 16), (1, 16)))
    kept_ranks = touch_ends(jax.random.randint(splits[6], (ROWS, COLS), CHI // 2, CHI + 1), jax.random.fold_in(splits[6], 1), CHI // 2, CHI).astype(jnp.int32)
    return dict(start_rows=start_rows, initial=initial, site_tensors=site_tensors, charges=charges, right_proj=right_proj, left_proj=left_proj, kept_ranks=kept_ranks)


def site_operator(tensor, charge):
    total = (charge[0][:, None, None, None] + charge[1][None, :, None, None]
             - charge[2][None, None, :, None] - charge[3][None, None, None, :])
    allowed = jnp.mod(total, 3) == 0
    return jnp.where(allowed, tensor.reshape(D, D, D, D), jnp.zeros((), tensor.dtype))


def keep_rank(projector, kept):
    inside = jnp.arange(CHI, dtype=jnp.int32) < kept
    return jnp.where(inside, projector, jnp.zeros((), projector.dtype))


def absorb_column(packed):
    boundary, operator, right, left = packed
    half_right = jnp.einsum('aub,bsk->ausk', boundary.astype(jnp.float32), right.astype(jnp.float32)).astype(jnp.bfloat16)
    with_sites = jnp.einsum('ludv,auvk->aldk', operator.astype(jnp.float32), half_right.astype(jnp.float32)).astype(jnp.bfloat16)
    return jnp.einsum('alm,aldk->mdk', left.astype(jnp.float32), with_sites.astype(jnp.float32)).astype(jnp.bfloat16)


def reference(start_rows, initial, site_tensors, charges, right_proj, left_proj, kept_ranks):
    operators = jax.vmap(jax.vmap(site_operator))(site_tensors, charges)
    kept_right = keep_rank(right_proj, kept_ranks[:, :, None, None, None])
    kept_left = keep_rank(left_proj, kept_ranks[:, :, None, None, None])
    left_in = jnp.roll(kept_left, 1, axis=1)
    absorbed = jnp.zeros((ROWS, COLS, CHI, D, CHI), jnp.bfloat16)
    for env_index in range(ENVS):
        boundary = initial[env_index]
        for step in range(ABSORB):
            row_index = (start_rows[env_index] + step).astype(jnp.int32)
            operator = lax.dynamic_index_in_dim(operators, row_index, 0, keepdims=False)
            right_now = lax.dynamic_index_in_dim(kept_right, row_index, 0, keepdims=False)
            left_now = lax.dynamic_index_in_dim(left_in, row_index, 0, keepdims=False)
            boundary = lax.map(absorb_column, (boundary, operator, right_now, left_now))
        last_row = (start_rows[env_index] + ABSORB - 1).astype(jnp.int32)
        absorbed = lax.dynamic_update_index_in_dim(absorbed, boundary, last_row, 0)
    return absorbed
```

```python
import functools

import jax
import jax.numpy as jnp
from jax import lax
from jax.experimental import pallas as pl
from jax.experimental.pallas import tpu as pltpu
from jax.sharding import PartitionSpec as P

ABSORB = 3
CHUNKS = 8
MESH = pl.DeviceIdType.MESH
BF16 = jnp.bfloat16
F32 = jnp.float32


def dot(a, b):
    return lax.dot_general(a, b, (((1,), (0,)), ((), ())), preferred_element_type=F32)


def dot_t(a, b):
    return lax.dot_general(a, b, (((1,), (1,)), ((), ())), preferred_element_type=F32)


def iota(shape, dim):
    return lax.broadcasted_iota(jnp.int32, shape, dim)


def block_operator(tensor_ref, charges_ref, inner, group):
    wide = inner * inner * inner
    row = iota((inner, wide), 0)
    col = iota((inner, wide), 1)
    up, down, right = col // (inner * inner), (col // inner) % inner, col % inner
    flat = tensor_ref[...].astype(F32)
    value = jnp.zeros((inner, wide), F32)
    total = jnp.zeros((inner, wide), jnp.int32)
    for v in range(inner):
        value = jnp.where(row == v, flat[:, v * wide : (v + 1) * wide], value)
        total = total + jnp.where(row == v, charges_ref[0, v], 0)
        total = total + jnp.where(up == v, charges_ref[1, v], 0)
        total = total - jnp.where(down == v, charges_ref[2, v], 0)
        total = total - jnp.where(right == v, charges_ref[3, v], 0)
    total = total + 6
    value = jnp.where(total % 3 == 0, value, 0.0)
    block = inner * group
    full = inner * block
    tiled = jnp.concatenate([value] * (full // inner), axis=0)
    down_of_row = iota((full, wide), 0) // block
    down_of_col = (iota((full, wide), 1) // inner) % inner
    tiled = jnp.where(down_of_row == down_of_col, tiled, 0.0).astype(BF16)
    src, dst = iota((wide, full), 0), iota((wide, full), 1)
    same_up = src // (inner * inner) == dst % inner
    same_right = src % inner == dst // block
    pick = jnp.where(same_up & same_right, 1.0, 0.0).astype(BF16)
    spread = dot(tiled, pick)
    a_row = (iota((full, full), 0) // inner) % group
    a_col = (iota((full, full), 1) // inner) % group
    return jnp.where(a_row == a_col, spread, 0.0)


def kernel(
    outer,
    inner,
    envs,
    start_ref,
    kept_ref,
    charges_ref,
    tensor_ref,
    initial_hbm,
    right_hbm,
    left_hbm,
    out_hbm,
    initial_v,
    raw,
    right_v,
    left_own,
    left_in,
    half,
    sites,
    acc,
    operator,
    outgoing,
    arrived,
    load_sem,
    left_send,
    left_recv,
    send_sem,
    recv_sem,
    store_sem,
):
    rows, cols = lax.axis_size("row"), lax.axis_size("col")
    row, col = lax.axis_index("row"), lax.axis_index("col")
    right_col = lax.rem(col + 1, cols)
    left_col = lax.rem(col + cols - 1, cols)
    size = outer * inner
    part = size // CHUNKS
    keys = outer // CHUNKS
    full = outer
    group = full // (inner * inner)
    groups = keys // group
    block = group * inner
    has_next = row < rows - 1
    has_before = row > 0

    load_left = pltpu.make_async_copy(left_hbm, raw.at[0], load_sem.at[0])
    load_right = pltpu.make_async_copy(right_hbm, raw.at[1], load_sem.at[1])
    load_initial = pltpu.make_async_copy(initial_hbm, initial_v, load_sem.at[2])
    load_left.start()
    load_right.start()
    load_initial.start()

    barrier = pltpu.get_barrier_semaphore()
    pl.semaphore_signal(barrier, inc=1, device_id=(row, right_col), device_id_type=MESH)
    pl.semaphore_signal(barrier, inc=1, device_id=(row, left_col), device_id_type=MESH)

    @pl.when(has_next)
    def _():
        pl.semaphore_signal(barrier, inc=1, device_id=(row + 1, col), device_id_type=MESH)

    @pl.when(has_before)
    def _():
        pl.semaphore_signal(barrier, inc=1, device_id=(row - 1, col), device_id_type=MESH)

    kept = kept_ref[0, 0]

    load_left.wait()
    kk = iota((full, full), 0)
    keep_eye = jnp.where((kk == iota((full, full), 1)) & (kk < kept), 1.0, 0.0).astype(BF16)
    for i in range(CHUNKS):
        left_own[i] = dot_t(keep_eye, raw[0, i * part : (i + 1) * part, :]).astype(BF16)

    pl.semaphore_wait(barrier, 2 + jnp.where(has_next, 1, 0) + jnp.where(has_before, 1, 0))

    def left_copy(i):
        span = pl.ds(i * keys, keys)
        return pltpu.make_async_remote_copy(
            src_ref=left_own.at[:, span, :],
            dst_ref=left_in.at[:, span, :],
            send_sem=left_send.at[i],
            recv_sem=left_recv.at[i],
            device_id=(row, right_col),
            device_id_type=MESH,
        )

    for i in range(CHUNKS):
        left_copy(i).start()

    def boundary_copy(step, i):
        span = pl.ds(i * part, part)
        return pltpu.make_async_remote_copy(
            src_ref=outgoing.at[step, span, :],
            dst_ref=arrived.at[step, span, :],
            send_sem=send_sem.at[step, i],
            recv_sem=recv_sem.at[step, i],
            device_id=(row + 1, col),
            device_id_type=MESH,
        )

    load_right.wait()
    to = iota((full, full), 0)
    frm = iota((full, full), 1)
    split = jnp.where(frm == (to % keys) * inner + to // keys, 1.0, 0.0).astype(BF16)
    merge = jnp.where(frm == (to % inner) * keys + to // inner, 1.0, 0.0).astype(BF16)
    inside = iota((full, full), 1) < kept
    for i in range(CHUNKS):
        moved = dot(split, raw[1, i * part : (i + 1) * part, :])
        moved = jnp.where(inside, moved, 0.0).astype(BF16)
        right_v[:, i * keys : (i + 1) * keys, :] = moved.reshape(inner, keys, full)

    operator[...] = block_operator(tensor_ref, charges_ref, inner, group).astype(BF16)

    @pl.when(jnp.logical_not(has_before))
    def _():
        arrived[...] = jnp.zeros_like(arrived)

    def absorb_sites(x, op_ref, i):
        for s in range(inner):
            half[s] = dot(x, right_v[s]).astype(BF16)
        for g in range(groups):
            piece = half[:, g * block : (g + 1) * block, :].reshape(full, full)
            made = dot(op_ref[...], piece).astype(BF16).reshape(inner, block, full)
            sites[:, pl.ds(i * part + g * block, block), :] = made

    load_initial.wait()

    def first(i, carry):
        x = jnp.zeros((part, outer), F32)
        for e in range(envs):
            here = jnp.full((part, outer), start_ref[e], jnp.int32) == row
            span = pl.ds(pl.multiple_of(e * size + i * part, part), part)
            x = jnp.where(here, initial_v[span, :].astype(F32), x)
        absorb_sites(x.astype(BF16), operator, i)
        return carry

    lax.fori_loop(0, CHUNKS, first, 0)

    def first_out(i, carry):
        left_copy(i).wait_recv()
        span = pl.ds(i * keys, keys)
        made = []
        for d in range(inner):
            total = dot(left_in[0, span, :], sites[d, 0:part, :])
            for c in range(1, CHUNKS):
                total += dot(left_in[c, span, :], sites[d, c * part : (c + 1) * part, :])
            made.append(total.astype(BF16))
        stacked = jnp.concatenate(made, axis=0)
        outgoing[0, pl.ds(i * part, part), :] = dot(merge, stacked).astype(BF16)

        @pl.when(has_next)
        def _():
            boundary_copy(0, i).start()

        return carry

    lax.fori_loop(0, CHUNKS, first_out, 0)

    for step in range(1, ABSORB):
        acc[...] = jnp.zeros_like(acc)

        def take(i, carry, step=step):
            @pl.when(has_before)
            def _():
                boundary_copy(step - 1, i).wait_recv()

            span = pl.ds(pl.multiple_of(i * part, part), part)
            absorb_sites(arrived[step - 1, span, :], operator, i)
            for d in range(inner):
                acc[d] += dot(left_in[i], sites[d, span, :])
            return carry

        lax.fori_loop(0, CHUNKS, take, 0)

        def give(i, carry, step=step):
            span = pl.ds(pl.multiple_of(i * keys, keys), keys)
            stacked = acc[:, span, :].astype(BF16).reshape(full, full)
            at = pl.ds(pl.multiple_of(i * part, part), part)
            outgoing[step, at, :] = dot(merge, stacked).astype(BF16)
            if step < ABSORB - 1:

                @pl.when(has_next)
                def _():
                    boundary_copy(step, i).start()

            else:
                pltpu.make_async_copy(outgoing.at[step, at, :], out_hbm.at[at, :], store_sem.at[i]).start()
            return carry

        lax.fori_loop(0, CHUNKS, give, 0)

    def finish(i, carry):
        left_copy(i).wait_send()

        @pl.when(has_next)
        def _():
            for step in range(ABSORB - 1):
                boundary_copy(step, i).wait_send()

        at = pl.ds(pl.multiple_of(i * part, part), part)
        pltpu.make_async_copy(outgoing.at[ABSORB - 1, at, :], out_hbm.at[at, :], store_sem.at[i]).wait()
        return carry

    lax.fori_loop(0, CHUNKS, finish, 0)


def shards(start_rows, initial, site_tensors, charges, right_proj, left_proj, kept_ranks):
    envs, _, outer, inner, _ = initial.shape
    size = outer * inner
    smem = pl.BlockSpec(memory_space=pltpu.SMEM)
    vmem = pl.BlockSpec(memory_space=pltpu.VMEM)
    hbm = pl.BlockSpec(memory_space=pl.ANY)
    out = pl.pallas_call(
        functools.partial(kernel, outer, inner, envs),
        out_shape=jax.ShapeDtypeStruct((size, outer), BF16),
        in_specs=[smem, smem, smem, vmem, hbm, hbm, hbm],
        out_specs=hbm,
        scratch_shapes=[
            pltpu.VMEM((envs * size, outer), BF16),
            pltpu.VMEM((2, size, outer), BF16),
            pltpu.VMEM((inner, outer, outer), BF16),
            pltpu.VMEM((CHUNKS, outer, size // CHUNKS), BF16),
            pltpu.VMEM((CHUNKS, outer, size // CHUNKS), BF16),
            pltpu.VMEM((inner, size // CHUNKS, outer), BF16),
            pltpu.VMEM((inner, size, outer), BF16),
            pltpu.VMEM((inner, outer, outer), F32),
            pltpu.VMEM((outer, outer), BF16),
            pltpu.VMEM((ABSORB, size, outer), BF16),
            pltpu.VMEM((ABSORB - 1, size, outer), BF16),
            pltpu.SemaphoreType.DMA((3,)),
            pltpu.SemaphoreType.DMA((CHUNKS,)),
            pltpu.SemaphoreType.DMA((CHUNKS,)),
            pltpu.SemaphoreType.DMA((ABSORB - 1, CHUNKS)),
            pltpu.SemaphoreType.DMA((ABSORB - 1, CHUNKS)),
            pltpu.SemaphoreType.DMA((CHUNKS,)),
        ],
        compiler_params=pltpu.CompilerParams(
            collective_id=0, has_side_effects=True, vmem_limit_bytes=56 * 1024 * 1024
        ),
        cost_estimate=pl.CostEstimate(
            flops=ABSORB * 6 * size * size * outer, bytes_accessed=8 * size * outer * 2, transcendentals=0
        ),
    )(
        start_rows,
        kept_ranks,
        charges[0, 0],
        site_tensors[0],
        initial.reshape(envs * size, outer),
        right_proj.reshape(size, outer),
        left_proj.reshape(size, outer),
    )
    return out.reshape(1, 1, outer, inner, outer)


def solution(mesh):
    return jax.shard_map(
        shards,
        mesh=mesh,
        in_specs=(
            P(),
            P(None, "col", None, None, None),
            P("row", "col", None),
            P("row", "col", None, None),
            P("row", "col", None, None, None),
            P("row", "col", None, None, None),
            P("row", "col"),
        ),
        out_specs=P("row", "col", None, None, None),
        check_vma=False,
    )
```

```python
import functools

import jax
import jax.numpy as jnp
from jax import lax
from jax.experimental import pallas as pl
from jax.experimental.pallas import tpu as pltpu
from jax.sharding import PartitionSpec as P

ABSORB = 3
CHUNKS = 8
LEFT_PARTS = 4
MESH = pl.DeviceIdType.MESH
BF16 = jnp.bfloat16
F32 = jnp.float32


def dot(a, b):
    return lax.dot_general(a, b, (((1,), (0,)), ((), ())), preferred_element_type=F32)


def dot_t(a, b):
    return lax.dot_general(a, b, (((1,), (1,)), ((), ())), preferred_element_type=F32)


def iota(shape, dim):
    return lax.broadcasted_iota(jnp.int32, shape, dim)


def block_operator(tensor_ref, charges_ref, inner, group):
    wide = inner * inner * inner
    row = iota((inner, wide), 0)
    col = iota((inner, wide), 1)
    up, down, right = col // (inner * inner), (col // inner) % inner, col % inner
    flat = tensor_ref[...].astype(F32)
    value = jnp.zeros((inner, wide), F32)
    total = jnp.zeros((inner, wide), jnp.int32)
    for v in range(inner):
        value = jnp.where(row == v, flat[:, v * wide : (v + 1) * wide], value)
        total = total + jnp.where(row == v, charges_ref[0, v], 0)
        total = total + jnp.where(up == v, charges_ref[1, v], 0)
        total = total - jnp.where(down == v, charges_ref[2, v], 0)
        total = total - jnp.where(right == v, charges_ref[3, v], 0)
    total = total + 6
    value = jnp.where(total % 3 == 0, value, 0.0)
    block = inner * group
    full = inner * block
    tiled = jnp.concatenate([value] * (full // inner), axis=0)
    down_of_row = iota((full, wide), 0) // block
    down_of_col = (iota((full, wide), 1) // inner) % inner
    tiled = jnp.where(down_of_row == down_of_col, tiled, 0.0).astype(BF16)
    src, dst = iota((wide, full), 0), iota((wide, full), 1)
    same_up = src // (inner * inner) == dst % inner
    same_right = src % inner == dst // block
    pick = jnp.where(same_up & same_right, 1.0, 0.0).astype(BF16)
    spread = dot(tiled, pick)
    a_row = (iota((full, full), 0) // inner) % group
    a_col = (iota((full, full), 1) // inner) % group
    return jnp.where(a_row == a_col, spread, 0.0)


def kernel(
    outer,
    inner,
    envs,
    start_ref,
    kept_ref,
    charges_ref,
    tensor_ref,
    initial_hbm,
    right_hbm,
    left_hbm,
    out_ref,
    initial_v,
    chosen,
    raw,
    right_v,
    left_own,
    left_in,
    half,
    sites,
    acc,
    operator,
    outgoing,
    arrived,
    load_sem,
    initial_sem,
    left_send,
    left_recv,
    send_sem,
    recv_sem,
):
    rows, cols = lax.axis_size("row"), lax.axis_size("col")
    row, col = lax.axis_index("row"), lax.axis_index("col")
    right_col = lax.rem(col + 1, cols)
    left_col = lax.rem(col + cols - 1, cols)
    size = outer * inner
    part = size // CHUNKS
    keys = outer // CHUNKS
    full = outer
    lanes = full // 2
    group = full // (inner * inner)
    block = group * inner
    pairs = inner // 2
    has_next = row < rows - 1
    has_before = row > 0

    load_left = pltpu.make_async_copy(left_hbm, raw.at[0], load_sem.at[0])
    load_right = pltpu.make_async_copy(right_hbm, raw.at[1], load_sem.at[1])
    load_left.start()
    load_right.start()

    def load_initial(i):
        span = pl.ds(i * part, part)
        return pltpu.make_async_copy(initial_hbm.at[:, span, :], initial_v.at[:, span, :], initial_sem.at[i])

    for i in range(CHUNKS):
        load_initial(i).start()

    barrier = pltpu.get_barrier_semaphore()
    pl.semaphore_signal(barrier, inc=1, device_id=(row, right_col), device_id_type=MESH)
    pl.semaphore_signal(barrier, inc=1, device_id=(row, left_col), device_id_type=MESH)

    @pl.when(has_next)
    def _():
        pl.semaphore_signal(barrier, inc=1, device_id=(row + 1, col), device_id_type=MESH)

    @pl.when(has_before)
    def _():
        pl.semaphore_signal(barrier, inc=1, device_id=(row - 1, col), device_id_type=MESH)

    kept = kept_ref[0, 0]
    operator[...] = block_operator(tensor_ref, charges_ref, inner, group).astype(BF16)

    load_left.wait()
    to, frm = iota((full, full), 0), iota((full, full), 1)
    keep_eye = jnp.where((to == frm) & (to < kept), 1.0, 0.0).astype(BF16)
    for i in range(CHUNKS):
        left_own[:, i * part : (i + 1) * part] = dot_t(keep_eye, raw[0, i * part : (i + 1) * part, :]).astype(BF16)

    pl.semaphore_wait(barrier, 2 + jnp.where(has_next, 1, 0) + jnp.where(has_before, 1, 0))

    def left_copy(i):
        span = pl.ds(i * (outer // LEFT_PARTS), outer // LEFT_PARTS)
        return pltpu.make_async_remote_copy(
            src_ref=left_own.at[span, :],
            dst_ref=left_in.at[span, :],
            send_sem=left_send.at[i],
            recv_sem=left_recv.at[i],
            device_id=(row, right_col),
            device_id_type=MESH,
        )

    for i in range(LEFT_PARTS):
        left_copy(i).start()

    def boundary_copy(step, h, i):
        span = pl.ds(i * part, part)
        return pltpu.make_async_remote_copy(
            src_ref=outgoing.at[step, h, span, :],
            dst_ref=arrived.at[step, h, span, :],
            send_sem=send_sem.at[step, h, i],
            recv_sem=recv_sem.at[step, h, i],
            device_id=(row + 1, col),
            device_id_type=MESH,
        )

    load_right.wait()
    split = jnp.where(frm == (to % keys) * inner + to // keys, 1.0, 0.0).astype(BF16)
    merge = jnp.where(frm == (to % inner) * keys + to // inner, 1.0, 0.0).astype(BF16)
    inside = frm < kept
    for i in range(CHUNKS):
        moved = dot(split, raw[1, i * part : (i + 1) * part, :])
        moved = jnp.where(inside, moved, 0.0).astype(BF16)
        for s in range(inner):
            for h in range(2):
                right_v[h, s // 2, i * keys : (i + 1) * keys, (s % 2) * lanes : (s % 2 + 1) * lanes] = moved[
                    s * keys : (s + 1) * keys, h * lanes : (h + 1) * lanes
                ]

    def absorb_sites(x, h, i):
        for p in range(pairs):
            y = dot(x, right_v[h, p]).astype(BF16)
            half[h, 2 * p] = y[:, :lanes]
            half[h, 2 * p + 1] = y[:, lanes:]
        for g in range(0, keys // group, 2):
            sides = [half[h, :, (g + n) * block : (g + n + 1) * block, :].reshape(full, lanes) for n in range(2)]
            y = dot(operator[...], jnp.concatenate(sides, axis=1)).astype(BF16)
            for d in range(inner):
                for n in range(2):
                    sites[h, d // 2, pl.ds(i * part + (g + n) * block, block), (d % 2) * lanes : (d % 2 + 1) * lanes] = y[
                        d * block : (d + 1) * block, n * lanes : (n + 1) * lanes
                    ]

    def merged(h, i):
        span = pl.ds(i * keys, keys)
        stacked = [acc[h, d // 2, span, (d % 2) * lanes : (d % 2 + 1) * lanes] for d in range(inner)]
        return dot(merge, jnp.concatenate(stacked, axis=0).astype(BF16)).astype(BF16)

    flags = [jnp.where(start_ref[e] == row, 1.0, 0.0) for e in range(envs)]

    def choose(i, carry):
        load_initial(i).wait()
        span = pl.ds(pl.multiple_of(i * part, part), part)
        x = initial_v[0, span, :] * jnp.full((part, outer), flags[0], F32).astype(BF16)
        for e in range(1, envs):
            x = x + initial_v[e, span, :] * jnp.full((part, outer), flags[e], F32).astype(BF16)
        chosen[span, :] = x
        absorb_sites(x, 0, i)
        return carry

    lax.fori_loop(0, CHUNKS, choose, 0)

    def give_first(h):
        for p in range(pairs):
            acc[h, p] = dot(left_in[...], sites[h, p])
        for i in range(CHUNKS):
            outgoing[0, h, i * part : (i + 1) * part, :] = merged(h, i)

            @pl.when(has_next)
            def _(i=i):
                boundary_copy(0, h, i).start()

    for i in range(LEFT_PARTS):
        left_copy(i).wait_recv()
    give_first(0)

    def second(i, carry):
        span = pl.ds(pl.multiple_of(i * part, part), part)
        absorb_sites(chosen[span, :], 1, i)
        return carry

    lax.fori_loop(0, CHUNKS, second, 0)
    give_first(1)

    @pl.when(jnp.logical_not(has_before))
    def _():
        arrived[...] = jnp.zeros_like(arrived)

    for step in range(1, ABSORB):

        def take(i, carry, step=step):
            @pl.when(has_before)
            def _():
                for h in range(2):
                    boundary_copy(step - 1, h, i).wait_recv()

            span = pl.ds(pl.multiple_of(i * part, part), part)
            x = jnp.concatenate([arrived[step - 1, h, span, :] for h in range(2)], axis=1)
            for h in range(2):
                absorb_sites(x, h, i)
            for h in range(2):
                for p in range(pairs):
                    acc[h, p] += dot(left_in[:, span], sites[h, p, span, :])
            return carry

        acc[...] = jnp.zeros_like(acc)
        lax.fori_loop(0, CHUNKS, take, 0)

        for i in range(CHUNKS):
            for h in range(2):
                if step < ABSORB - 1:
                    outgoing[step, h, i * part : (i + 1) * part, :] = merged(h, i)

                    @pl.when(has_next)
                    def _(i=i, h=h, step=step):
                        boundary_copy(step, h, i).start()

                else:
                    out_ref[i * part : (i + 1) * part, h * lanes : (h + 1) * lanes] = merged(h, i)

    for i in range(LEFT_PARTS):
        left_copy(i).wait_send()

    @pl.when(has_next)
    def _():
        for step in range(ABSORB - 1):
            for h in range(2):
                for i in range(CHUNKS):
                    boundary_copy(step, h, i).wait_send()


def shards(start_rows, initial, site_tensors, charges, right_proj, left_proj, kept_ranks):
    envs, _, outer, inner, _ = initial.shape
    size = outer * inner
    smem = pl.BlockSpec(memory_space=pltpu.SMEM)
    vmem = pl.BlockSpec(memory_space=pltpu.VMEM)
    hbm = pl.BlockSpec(memory_space=pl.ANY)
    out = pl.pallas_call(
        functools.partial(kernel, outer, inner, envs),
        out_shape=jax.ShapeDtypeStruct((size, outer), BF16),
        in_specs=[smem, smem, smem, vmem, hbm, hbm, hbm],
        out_specs=vmem,
        scratch_shapes=[
            pltpu.VMEM((envs, size, outer), BF16),
            pltpu.VMEM((size, outer), BF16),
            pltpu.VMEM((2, size, outer), BF16),
            pltpu.VMEM((2, inner // 2, outer, outer), BF16),
            pltpu.VMEM((outer, size), BF16),
            pltpu.VMEM((outer, size), BF16),
            pltpu.VMEM((2, inner, size // CHUNKS, outer // 2), BF16),
            pltpu.VMEM((2, inner // 2, size, outer), BF16),
            pltpu.VMEM((2, inner // 2, outer, outer), F32),
            pltpu.VMEM((outer, outer), BF16),
            pltpu.VMEM((ABSORB - 1, 2, size, outer // 2), BF16),
            pltpu.VMEM((ABSORB - 1, 2, size, outer // 2), BF16),
            pltpu.SemaphoreType.DMA((2,)),
            pltpu.SemaphoreType.DMA((CHUNKS,)),
            pltpu.SemaphoreType.DMA((LEFT_PARTS,)),
            pltpu.SemaphoreType.DMA((LEFT_PARTS,)),
            pltpu.SemaphoreType.DMA((ABSORB - 1, 2, CHUNKS)),
            pltpu.SemaphoreType.DMA((ABSORB - 1, 2, CHUNKS)),
        ],
        compiler_params=pltpu.CompilerParams(
            collective_id=0, has_side_effects=True, vmem_limit_bytes=56 * 1024 * 1024
        ),
        cost_estimate=pl.CostEstimate(
            flops=ABSORB * 6 * size * size * outer, bytes_accessed=8 * size * outer * 2, transcendentals=0
        ),
    )(
        start_rows,
        kept_ranks,
        charges[0, 0],
        site_tensors[0],
        initial.reshape(envs, size, outer),
        right_proj.reshape(size, outer),
        left_proj.reshape(size, outer),
    )
    return out.reshape(1, 1, outer, inner, outer)


def solution(mesh):
    return jax.shard_map(
        shards,
        mesh=mesh,
        in_specs=(
            P(),
            P(None, "col", None, None, None),
            P("row", "col", None),
            P("row", "col", None, None),
            P("row", "col", None, None, None),
            P("row", "col", None, None, None),
            P("row", "col"),
        ),
        out_specs=P("row", "col", None, None, None),
        check_vma=False,
    )
```

```python
import functools

import jax
import jax.numpy as jnp
from jax import lax
from jax.experimental import pallas as pl
from jax.experimental.pallas import tpu as pltpu
from jax.sharding import PartitionSpec as P

ABSORB = 3
CHUNKS = 8
LEFT_PARTS = 4
MESH = pl.DeviceIdType.MESH
BF16 = jnp.bfloat16
F32 = jnp.float32


def dot(a, b):
    return lax.dot_general(a, b, (((1,), (0,)), ((), ())), preferred_element_type=F32)


def dot_t(a, b):
    return lax.dot_general(a, b, (((1,), (1,)), ((), ())), preferred_element_type=F32)


def iota(shape, dim):
    return lax.broadcasted_iota(jnp.int32, shape, dim)


def block_operator(tensor_ref, charges_ref, inner, group):
    wide = inner * inner * inner
    row = iota((inner, wide), 0)
    col = iota((inner, wide), 1)
    up, down, right = col // (inner * inner), (col // inner) % inner, col % inner
    flat = tensor_ref[...].astype(F32)
    value = jnp.zeros((inner, wide), F32)
    total = jnp.zeros((inner, wide), jnp.int32)
    for v in range(inner):
        value = jnp.where(row == v, flat[:, v * wide : (v + 1) * wide], value)
        total = total + jnp.where(row == v, charges_ref[0, v], 0)
        total = total + jnp.where(up == v, charges_ref[1, v], 0)
        total = total - jnp.where(down == v, charges_ref[2, v], 0)
        total = total - jnp.where(right == v, charges_ref[3, v], 0)
    total = total + 6
    value = jnp.where(total % 3 == 0, value, 0.0)
    block = inner * group
    full = inner * block
    tiled = jnp.concatenate([value] * (full // inner), axis=0)
    down_of_row = iota((full, wide), 0) // block
    down_of_col = (iota((full, wide), 1) // inner) % inner
    tiled = jnp.where(down_of_row == down_of_col, tiled, 0.0).astype(BF16)
    src, dst = iota((wide, full), 0), iota((wide, full), 1)
    same_up = src // (inner * inner) == dst % inner
    same_right = src % inner == dst // block
    pick = jnp.where(same_up & same_right, 1.0, 0.0).astype(BF16)
    spread = dot(tiled, pick)
    a_row = (iota((full, full), 0) // inner) % group
    a_col = (iota((full, full), 1) // inner) % group
    return jnp.where(a_row == a_col, spread, 0.0)


def kernel(
    outer,
    inner,
    envs,
    start_ref,
    kept_ref,
    charges_ref,
    tensor_hbm,
    initial_hbm,
    right_hbm,
    left_hbm,
    out_ref,
    tensor_ref,
    initial_v,
    chosen,
    raw,
    right_v,
    left_own,
    left_in,
    half,
    sites,
    acc,
    operator,
    outgoing,
    arrived,
    load_sem,
    initial_sem,
    left_send,
    left_recv,
    send_sem,
    recv_sem,
):
    rows, cols = lax.axis_size("row"), lax.axis_size("col")
    row, col = lax.axis_index("row"), lax.axis_index("col")
    right_col = lax.rem(col + 1, cols)
    left_col = lax.rem(col + cols - 1, cols)
    size = outer * inner
    part = size // CHUNKS
    keys = outer // CHUNKS
    full = outer
    lanes = full // 2
    group = full // (inner * inner)
    block = group * inner
    pairs = inner // 2
    has_next = row < rows - 1
    has_before = row > 0

    load_left = pltpu.make_async_copy(left_hbm, raw.at[0], load_sem.at[0])
    load_right = pltpu.make_async_copy(right_hbm, raw.at[1], load_sem.at[1])
    load_left.start()
    load_right.start()
    load_tensor = pltpu.make_async_copy(tensor_hbm, tensor_ref, load_sem.at[2])
    load_tensor.start()

    def load_initial(i):
        span = pl.ds(i * 2 * part, 2 * part)
        return pltpu.make_async_copy(initial_hbm.at[:, span, :], initial_v.at[:, span, :], initial_sem.at[i])

    barrier = pltpu.get_barrier_semaphore()
    pl.semaphore_signal(barrier, inc=1, device_id=(row, left_col), device_id_type=MESH)

    @pl.when(has_before)
    def _():
        pl.semaphore_signal(barrier, inc=1, device_id=(row - 1, col), device_id_type=MESH)

    kept = kept_ref[0, 0]
    load_tensor.wait()
    operator[...] = block_operator(tensor_ref, charges_ref, inner, group).astype(BF16)

    load_left.wait()
    for i in range(CHUNKS // 2):
        load_initial(i).start()
    to, frm = iota((full, full), 0), iota((full, full), 1)
    keep_eye = jnp.where((to == frm) & (to < kept), 1.0, 0.0).astype(BF16)
    for i in range(CHUNKS):
        left_own[:, i * part : (i + 1) * part] = dot_t(keep_eye, raw[0, i * part : (i + 1) * part, :]).astype(BF16)

    pl.semaphore_wait(barrier, 1 + jnp.where(has_next, 1, 0))

    def left_copy(i):
        span = pl.ds(i * (outer // LEFT_PARTS), outer // LEFT_PARTS)
        return pltpu.make_async_remote_copy(
            src_ref=left_own.at[span, :],
            dst_ref=left_in.at[span, :],
            send_sem=left_send.at[i],
            recv_sem=left_recv.at[i],
            device_id=(row, right_col),
            device_id_type=MESH,
        )

    for i in range(LEFT_PARTS):
        left_copy(i).start()

    def boundary_copy(step, h, i):
        span = pl.ds(i * part, part)
        return pltpu.make_async_remote_copy(
            src_ref=outgoing.at[step, h, span, :],
            dst_ref=arrived.at[step, h, span, :],
            send_sem=send_sem.at[step, h, i],
            recv_sem=recv_sem.at[step, h, i],
            device_id=(row + 1, col),
            device_id_type=MESH,
        )

    load_right.wait()
    split = jnp.where(frm == (to % keys) * inner + to // keys, 1.0, 0.0).astype(BF16)
    merge = jnp.where(frm == (to % inner) * keys + to // inner, 1.0, 0.0).astype(BF16)
    inside = frm < kept
    for i in range(CHUNKS):
        moved = dot(split, raw[1, i * part : (i + 1) * part, :])
        moved = jnp.where(inside, moved, 0.0).astype(BF16)
        for s in range(inner):
            for h in range(2):
                right_v[h, s // 2, i * keys : (i + 1) * keys, (s % 2) * lanes : (s % 2 + 1) * lanes] = moved[
                    s * keys : (s + 1) * keys, h * lanes : (h + 1) * lanes
                ]

    def absorb_sites(x, h, at):
        count = x.shape[0]
        for p in range(pairs):
            y = dot(x, right_v[h, p]).astype(BF16)
            half[h, 2 * p, :count] = y[:, :lanes]
            half[h, 2 * p + 1, :count] = y[:, lanes:]
        for g in range(0, count // block, 2):
            sides = [half[h, :, (g + n) * block : (g + n + 1) * block, :].reshape(full, lanes) for n in range(2)]
            y = dot(operator[...], jnp.concatenate(sides, axis=1)).astype(BF16)
            for d in range(inner):
                for n in range(2):
                    sites[h, d // 2, pl.ds(at + (g + n) * block, block), (d % 2) * lanes : (d % 2 + 1) * lanes] = y[
                        d * block : (d + 1) * block, n * lanes : (n + 1) * lanes
                    ]

    def merged(h, i):
        span = pl.ds(i * keys, keys)
        stacked = [acc[h, d // 2, span, (d % 2) * lanes : (d % 2 + 1) * lanes] for d in range(inner)]
        return dot(merge, jnp.concatenate(stacked, axis=0).astype(BF16)).astype(BF16)

    flags = [jnp.where(start_ref[e] == row, 1.0, 0.0) for e in range(envs)]

    def choose(i, carry):
        load_initial(i).wait()
        at = pl.multiple_of(i * 2 * part, 2 * part)
        span = pl.ds(at, 2 * part)
        x = initial_v[0, span, :] * jnp.full((2 * part, outer), flags[0], F32).astype(BF16)
        for e in range(1, envs):
            x = x + initial_v[e, span, :] * jnp.full((2 * part, outer), flags[e], F32).astype(BF16)
        chosen[span, :] = x
        absorb_sites(x, 0, at)
        return carry

    lax.fori_loop(0, CHUNKS // 2, choose, 0)

    def give_first(h):
        for p in range(pairs):
            acc[h, p] = dot(left_in[...], sites[h, p])
        for i in range(CHUNKS):
            outgoing[0, h, i * part : (i + 1) * part, :] = merged(h, i)

            @pl.when(has_next)
            def _(i=i):
                boundary_copy(0, h, i).start()

    for i in range(LEFT_PARTS):
        left_copy(i).wait_recv()
    give_first(0)

    def second(i, carry):
        at = pl.multiple_of(i * 2 * part, 2 * part)
        absorb_sites(chosen[pl.ds(at, 2 * part), :], 1, at)
        return carry

    lax.fori_loop(0, CHUNKS // 2, second, 0)
    give_first(1)

    @pl.when(jnp.logical_not(has_before))
    def _():
        arrived[...] = jnp.zeros_like(arrived)

    for step in range(1, ABSORB):

        def take(i, carry, step=step, count=2):
            @pl.when(has_before)
            def _():
                for n in range(count):
                    for h in range(2):
                        boundary_copy(step - 1, h, i * count + n).wait_recv()

            at = pl.multiple_of(i * count * part, count * part)
            span = pl.ds(at, count * part)
            x = jnp.concatenate([arrived[step - 1, h, span, :] for h in range(2)], axis=1)
            for h in range(2):
                absorb_sites(x, h, at)
            for h in range(2):
                for p in range(pairs):
                    acc[h, p] += dot(left_in[:, span], sites[h, p, span, :])
            return carry

        acc[...] = jnp.zeros_like(acc)
        lax.fori_loop(0, CHUNKS // 2 - 1, take, 0)
        lax.fori_loop(CHUNKS - 2, CHUNKS, functools.partial(take, count=1), 0)

        for i in range(CHUNKS):
            if step < ABSORB - 1:
                for h in range(2):
                    outgoing[step, h, i * part : (i + 1) * part, :] = merged(h, i)

                    @pl.when(has_next)
                    def _(i=i, h=h, step=step):
                        boundary_copy(step, h, i).start()

            else:
                out_ref[i * part : (i + 1) * part, :] = jnp.concatenate([merged(h, i) for h in range(2)], axis=1)

    for i in range(LEFT_PARTS):
        left_copy(i).wait_send()

    @pl.when(has_next)
    def _():
        for step in range(ABSORB - 1):
            for h in range(2):
                for i in range(CHUNKS):
                    boundary_copy(step, h, i).wait_send()


def shards(start_rows, initial, site_tensors, charges, right_proj, left_proj, kept_ranks):
    envs, _, outer, inner, _ = initial.shape
    size = outer * inner
    smem = pl.BlockSpec(memory_space=pltpu.SMEM)
    vmem = pl.BlockSpec(memory_space=pltpu.VMEM)
    hbm = pl.BlockSpec(memory_space=pltpu.HBM)
    out = pl.pallas_call(
        functools.partial(kernel, outer, inner, envs),
        out_shape=pltpu.VMEM((size, outer), BF16),
        in_specs=[smem, smem, smem, hbm, hbm, hbm, hbm],
        out_specs=vmem,
        scratch_shapes=[
            pltpu.VMEM((1, inner**4), BF16),
            pltpu.VMEM((envs, size, outer), BF16),
            pltpu.VMEM((size, outer), BF16),
            pltpu.VMEM((2, size, outer), BF16),
            pltpu.VMEM((2, inner // 2, outer, outer), BF16),
            pltpu.VMEM((outer, size), BF16),
            pltpu.VMEM((outer, size), BF16),
            pltpu.VMEM((2, inner, 2 * size // CHUNKS, outer // 2), BF16),
            pltpu.VMEM((2, inner // 2, size, outer), BF16),
            pltpu.VMEM((2, inner // 2, outer, outer), F32),
            pltpu.VMEM((outer, outer), BF16),
            pltpu.VMEM((ABSORB - 1, 2, size, outer // 2), BF16),
            pltpu.VMEM((ABSORB - 1, 2, size, outer // 2), BF16),
            pltpu.SemaphoreType.DMA((3,)),
            pltpu.SemaphoreType.DMA((CHUNKS // 2,)),
            pltpu.SemaphoreType.DMA((LEFT_PARTS,)),
            pltpu.SemaphoreType.DMA((LEFT_PARTS,)),
            pltpu.SemaphoreType.DMA((ABSORB - 1, 2, CHUNKS)),
            pltpu.SemaphoreType.DMA((ABSORB - 1, 2, CHUNKS)),
        ],
        compiler_params=pltpu.CompilerParams(
            collective_id=0, has_side_effects=True, vmem_limit_bytes=58 * 1024 * 1024
        ),
        cost_estimate=pl.CostEstimate(
            flops=ABSORB * 6 * size * size * outer, bytes_accessed=8 * size * outer * 2, transcendentals=0
        ),
    )(
        start_rows,
        kept_ranks,
        charges[0, 0],
        site_tensors[0],
        initial.reshape(envs, size, outer),
        right_proj.reshape(size, outer),
        left_proj.reshape(size, outer),
    )
    return out.reshape(1, 1, outer, inner, outer)


def solution(mesh):
    return jax.shard_map(
        shards,
        mesh=mesh,
        in_specs=(
            P(),
            P(None, "col", None, None, None),
            P("row", "col", None),
            P("row", "col", None, None),
            P("row", "col", None, None, None),
            P("row", "col", None, None, None),
            P("row", "col"),
        ),
        out_specs=P("row", "col", None, None, None),
        check_vma=False,
    )
```

```python
import functools

import jax
import jax.numpy as jnp
from jax import lax
from jax.experimental import pallas as pl
from jax.experimental.pallas import tpu as pltpu
from jax.sharding import PartitionSpec as P

ABSORB = 3
CHUNKS = 8
LEFT_PARTS = 4
MESH = pl.DeviceIdType.MESH
BF16 = jnp.bfloat16
F32 = jnp.float32


def dot(a, b):
    return lax.dot_general(a, b, (((1,), (0,)), ((), ())), preferred_element_type=F32)


def dot_t(a, b):
    return lax.dot_general(a, b, (((1,), (1,)), ((), ())), preferred_element_type=F32)


def iota(shape, dim):
    return lax.broadcasted_iota(jnp.int32, shape, dim)


def block_operator(tensor_ref, charges_ref, inner, group):
    wide = inner * inner * inner
    row = iota((inner, wide), 0)
    col = iota((inner, wide), 1)
    up, down, right = col // (inner * inner), (col // inner) % inner, col % inner
    flat = tensor_ref[...].astype(F32)
    value = jnp.zeros((inner, wide), F32)
    total = jnp.zeros((inner, wide), jnp.int32)
    for v in range(inner):
        value = jnp.where(row == v, flat[:, v * wide : (v + 1) * wide], value)
        total = total + jnp.where(row == v, charges_ref[0, v], 0)
        total = total + jnp.where(up == v, charges_ref[1, v], 0)
        total = total - jnp.where(down == v, charges_ref[2, v], 0)
        total = total - jnp.where(right == v, charges_ref[3, v], 0)
    total = total + 6
    value = jnp.where(total % 3 == 0, value, 0.0)
    block = inner * group
    full = inner * block
    tiled = jnp.concatenate([value] * (full // inner), axis=0)
    down_of_row = iota((full, wide), 0) // block
    down_of_col = (iota((full, wide), 1) // inner) % inner
    tiled = jnp.where(down_of_row == down_of_col, tiled, 0.0).astype(BF16)
    src, dst = iota((wide, full), 0), iota((wide, full), 1)
    same_up = src // (inner * inner) == dst % inner
    same_right = src % inner == dst // block
    pick = jnp.where(same_up & same_right, 1.0, 0.0).astype(BF16)
    spread = dot(tiled, pick)
    a_row = (iota((full, full), 0) // inner) % group
    a_col = (iota((full, full), 1) // inner) % group
    return jnp.where(a_row == a_col, spread, 0.0)


def kernel(
    outer,
    inner,
    envs,
    start_ref,
    kept_ref,
    charges_ref,
    tensor_hbm,
    initial_hbm,
    right_hbm,
    left_hbm,
    out_ref,
    tensor_ref,
    initial_v,
    chosen,
    raw,
    right_v,
    left_own,
    left_in,
    half,
    sites,
    acc,
    operator,
    outgoing,
    arrived,
    load_sem,
    initial_sem,
    left_send,
    left_recv,
    send_sem,
    recv_sem,
    passing,
    relay_send,
    relay_recv,
):
    rows, cols = lax.axis_size("row"), lax.axis_size("col")
    row, col = lax.axis_index("row"), lax.axis_index("col")
    right_col = lax.rem(col + 1, cols)
    left_col = lax.rem(col + cols - 1, cols)
    size = outer * inner
    part = size // CHUNKS
    keys = outer // CHUNKS
    full = outer
    lanes = full // 2
    group = full // (inner * inner)
    block = group * inner
    pairs = inner // 2

    def working(step):
        return (row >= step) & (row <= rows - ABSORB + step)

    cross = rows // 2 - 1
    crosses = row == cross
    relays = row == rows - 1
    lands = row == cross + 1
    far_col = lax.rem(col + cols // 2, cols)
    sends_any = row < rows - 1
    receives_any = row > 0
    odd = lax.rem(col, 2) == 1

    load_left = pltpu.make_async_copy(left_hbm, raw.at[0], load_sem.at[0])
    load_right = pltpu.make_async_copy(right_hbm, raw.at[1], load_sem.at[1])
    load_left.start()
    load_right.start()
    load_tensor = pltpu.make_async_copy(tensor_hbm, tensor_ref, load_sem.at[2])
    load_tensor.start()

    def load_initial(i):
        span = pl.ds(i * 2 * part, 2 * part)
        return pltpu.make_async_copy(initial_hbm.at[:, span, :], initial_v.at[:, span, :], initial_sem.at[i])

    load_initial(0).start()

    barrier = pltpu.get_barrier_semaphore()
    pl.semaphore_signal(barrier, inc=1, device_id=(row, left_col), device_id_type=MESH)

    @pl.when(receives_any)
    def _():
        pl.semaphore_signal(barrier, inc=1, device_id=(row - 1, col), device_id_type=MESH)

    @pl.when(relays)
    def _():
        pl.semaphore_signal(barrier, inc=1, device_id=(cross, far_col), device_id_type=MESH)

    @pl.when(lands)
    def _():
        pl.semaphore_signal(barrier, inc=1, device_id=(rows - 1, far_col), device_id_type=MESH)

    kept = kept_ref[0, 0]
    load_left.wait()
    load_initial(1).start()
    to, frm = iota((full, full), 0), iota((full, full), 1)
    keep_eye = jnp.where((to == frm) & (to < kept), 1.0, 0.0).astype(BF16)
    for i in range(CHUNKS):
        left_own[:, i * part : (i + 1) * part] = dot_t(keep_eye, raw[0, i * part : (i + 1) * part, :]).astype(BF16)

    def left_copy(i):
        span = pl.ds(i * (outer // LEFT_PARTS), outer // LEFT_PARTS)
        return pltpu.make_async_remote_copy(
            src_ref=left_own.at[span, :],
            dst_ref=left_in.at[span, :],
            send_sem=left_send.at[i],
            recv_sem=left_recv.at[i],
            device_id=(row, right_col),
            device_id_type=MESH,
        )

    pl.semaphore_wait(barrier, 1 + jnp.where(sends_any, 1, 0) + jnp.where(crosses, 1, 0) + jnp.where(relays, 1, 0))
    for i in range(LEFT_PARTS):
        left_copy(i).start()

    def boundary_copy(step, h, i):
        span = pl.ds(i * part, part)
        return pltpu.make_async_remote_copy(
            src_ref=outgoing.at[step, h, span, :],
            dst_ref=arrived.at[step, h, span, :],
            send_sem=send_sem.at[step, h, i],
            recv_sem=recv_sem.at[step, h, i],
            device_id=(row + 1, col),
            device_id_type=MESH,
        )

    def to_relay(step, i):
        span = pl.ds(i * part, part)
        return pltpu.make_async_remote_copy(
            src_ref=outgoing.at[step, 1, span, :],
            dst_ref=passing.at[step, span, :],
            send_sem=send_sem.at[step, 1, i],
            recv_sem=relay_recv.at[step, i],
            device_id=(rows - 1, far_col),
            device_id_type=MESH,
        )

    def from_relay(step, i):
        span = pl.ds(i * part, part)
        return pltpu.make_async_remote_copy(
            src_ref=passing.at[step, span, :],
            dst_ref=arrived.at[step, 1, span, :],
            send_sem=relay_send.at[step, i],
            recv_sem=recv_sem.at[step, 1, i],
            device_id=(cross + 1, far_col),
            device_id_type=MESH,
        )

    def pass_on(step, i):
        to_relay(step, i).wait_recv()
        from_relay(step, i).start()

    def give(step, h, i):
        if h == 0:
            boundary_copy(step, 0, i).start()
        else:

            @pl.when(crosses)
            def _():
                to_relay(step, i).start()

            @pl.when(jnp.logical_not(crosses))
            def _():
                boundary_copy(step, 1, i).start()

    load_tensor.wait()
    operator[...] = block_operator(tensor_ref, charges_ref, inner, group).astype(BF16)

    load_right.wait()
    split = jnp.where(frm == (to % keys) * inner + to // keys, 1.0, 0.0).astype(BF16)
    merge = jnp.where(frm == (to % inner) * keys + to // inner, 1.0, 0.0).astype(BF16)
    inside = frm < kept
    for i in range(CHUNKS):
        moved = dot(split, raw[1, i * part : (i + 1) * part, :])
        moved = jnp.where(inside, moved, 0.0).astype(BF16)
        for s in range(inner):
            for h in range(2):
                right_v[h, s // 2, i * keys : (i + 1) * keys, (s % 2) * lanes : (s % 2 + 1) * lanes] = moved[
                    s * keys : (s + 1) * keys, h * lanes : (h + 1) * lanes
                ]

    def absorb_sites(x, h, at):
        count = x.shape[0]
        for p in range(pairs):
            y = dot(x, right_v[h, p]).astype(BF16)
            half[h, 2 * p, :count] = y[:, :lanes]
            half[h, 2 * p + 1, :count] = y[:, lanes:]
        for g in range(0, count // block, 2):
            sides = [half[h, :, (g + n) * block : (g + n + 1) * block, :].reshape(full, lanes) for n in range(2)]
            y = dot(operator[...], jnp.concatenate(sides, axis=1)).astype(BF16)
            for d in range(inner):
                for n in range(2):
                    sites[h, d // 2, pl.ds(at + (g + n) * block, block), (d % 2) * lanes : (d % 2 + 1) * lanes] = y[
                        d * block : (d + 1) * block, n * lanes : (n + 1) * lanes
                    ]

    def merged(halves, i):
        span = pl.ds(i * keys, keys)
        sides = []
        for h in halves:
            stacked = [acc[h, d // 2, span, (d % 2) * lanes : (d % 2 + 1) * lanes] for d in range(inner)]
            sides.append(jnp.concatenate(stacked, axis=0).astype(BF16))
        return dot(merge, jnp.concatenate(sides, axis=1)).astype(BF16)

    flags = [jnp.where(start_ref[e] == row, 1.0, 0.0) for e in range(envs)]

    def choose(i, carry):
        load_initial(i).wait()

        @pl.when(i < CHUNKS // 2 - 2)
        def _():
            load_initial(i + 2).start()

        at = pl.multiple_of(i * 2 * part, 2 * part)
        span = pl.ds(at, 2 * part)
        x = initial_v[0, span, :] * jnp.full((2 * part, outer), flags[0], F32).astype(BF16)
        for e in range(1, envs):
            x = x + initial_v[e, span, :] * jnp.full((2 * part, outer), flags[e], F32).astype(BF16)
        chosen[span, :] = x
        absorb_sites(x, 0, at)
        return carry

    lax.fori_loop(0, CHUNKS // 2, choose, 0)

    def give_first(h):
        for p in range(pairs):
            acc[h, p] = dot(left_in[...], sites[h, p])
        for i in range(CHUNKS):
            outgoing[0, h, i * part : (i + 1) * part, :] = merged((h,), i)

            @pl.when(working(0))
            def _(i=i):
                give(0, h, i)

    @pl.when(relays)
    def _():
        for i in range(CHUNKS):
            pass_on(0, i)

    def second(i, carry):
        at = pl.multiple_of(i * 2 * part, 2 * part)
        absorb_sites(chosen[pl.ds(at, 2 * part), :], 1, at)
        return carry

    @pl.when(jnp.logical_not(odd))
    def _():
        lax.fori_loop(0, CHUNKS // 2, second, 0)

    for i in range(LEFT_PARTS):
        left_copy(i).wait_recv()
    give_first(0)

    @pl.when(odd)
    def _():
        lax.fori_loop(0, CHUNKS // 2, second, 0)

    give_first(1)

    def later(step):
        def take(i, carry, count=2):
            for n in range(count):
                for h in range(2):
                    boundary_copy(step - 1, h, i * count + n).wait_recv()

            at = pl.multiple_of(i * count * part, count * part)
            span = pl.ds(at, count * part)
            x = jnp.concatenate([arrived[step - 1, h, span, :] for h in range(2)], axis=1)
            for h in range(2):
                absorb_sites(x, h, at)
            for h in range(2):
                for p in range(pairs):
                    acc[h, p] += dot(left_in[:, span], sites[h, p, span, :])
            return carry

        if step == ABSORB - 1:

            @pl.when(relays)
            def _():
                for i in range(CHUNKS):
                    pass_on(step - 1, i)

        acc[...] = jnp.zeros_like(acc)
        lax.fori_loop(0, CHUNKS // 2 - 1, take, 0)
        lax.fori_loop(CHUNKS - 2, CHUNKS, functools.partial(take, count=1), 0)

        for i in range(CHUNKS):
            made = merged((0, 1), i)
            if step < ABSORB - 1:
                for h in range(2):
                    outgoing[step, h, i * part : (i + 1) * part, :] = made[:, h * lanes : (h + 1) * lanes]
                    give(step, h, i)
            else:
                out_ref[i * part : (i + 1) * part, :] = made

    for step in range(1, ABSORB):

        @pl.when(working(step))
        def _(step=step):
            later(step)

    @pl.when(jnp.logical_not(working(ABSORB - 1)))
    def _():
        out_ref[...] = jnp.zeros_like(out_ref)

    for i in range(LEFT_PARTS):
        left_copy(i).wait_send()

    for step in range(ABSORB - 1):

        @pl.when(working(step))
        def _(step=step):
            for h in range(2):
                for i in range(CHUNKS):
                    boundary_copy(step, h, i).wait_send()

        @pl.when(relays)
        def _(step=step):
            for i in range(CHUNKS):
                from_relay(step, i).wait_send()


def shards(start_rows, initial, site_tensors, charges, right_proj, left_proj, kept_ranks):
    envs, _, outer, inner, _ = initial.shape
    size = outer * inner
    smem = pl.BlockSpec(memory_space=pltpu.SMEM)
    vmem = pl.BlockSpec(memory_space=pltpu.VMEM)
    hbm = pl.BlockSpec(memory_space=pltpu.HBM)
    out = pl.pallas_call(
        functools.partial(kernel, outer, inner, envs),
        out_shape=pltpu.VMEM((size, outer), BF16),
        in_specs=[smem, smem, smem, hbm, hbm, hbm, hbm],
        out_specs=vmem,
        scratch_shapes=[
            pltpu.VMEM((1, inner**4), BF16),
            pltpu.VMEM((envs, size, outer), BF16),
            pltpu.VMEM((size, outer), BF16),
            pltpu.VMEM((2, size, outer), BF16),
            pltpu.VMEM((2, inner // 2, outer, outer), BF16),
            pltpu.VMEM((outer, size), BF16),
            pltpu.VMEM((outer, size), BF16),
            pltpu.VMEM((2, inner, 2 * size // CHUNKS, outer // 2), BF16),
            pltpu.VMEM((2, inner // 2, size, outer), BF16),
            pltpu.VMEM((2, inner // 2, outer, outer), F32),
            pltpu.VMEM((outer, outer), BF16),
            pltpu.VMEM((ABSORB - 1, 2, size, outer // 2), BF16),
            pltpu.VMEM((ABSORB - 1, 2, size, outer // 2), BF16),
            pltpu.SemaphoreType.DMA((3,)),
            pltpu.SemaphoreType.DMA((CHUNKS // 2,)),
            pltpu.SemaphoreType.DMA((LEFT_PARTS,)),
            pltpu.SemaphoreType.DMA((LEFT_PARTS,)),
            pltpu.SemaphoreType.DMA((ABSORB - 1, 2, CHUNKS)),
            pltpu.SemaphoreType.DMA((ABSORB - 1, 2, CHUNKS)),
            pltpu.VMEM((ABSORB - 1, size, outer // 2), BF16),
            pltpu.SemaphoreType.DMA((ABSORB - 1, CHUNKS)),
            pltpu.SemaphoreType.DMA((ABSORB - 1, CHUNKS)),
        ],
        compiler_params=pltpu.CompilerParams(
            collective_id=0, has_side_effects=True, vmem_limit_bytes=58 * 1024 * 1024
        ),
        cost_estimate=pl.CostEstimate(
            flops=ABSORB * 6 * size * size * outer, bytes_accessed=8 * size * outer * 2, transcendentals=0
        ),
    )(
        start_rows,
        kept_ranks,
        charges[0, 0],
        site_tensors[0],
        initial.reshape(envs, size, outer),
        right_proj.reshape(size, outer),
        left_proj.reshape(size, outer),
    )
    return out.reshape(1, 1, outer, inner, outer)


def solution(mesh):
    return jax.shard_map(
        shards,
        mesh=mesh,
        in_specs=(
            P(),
            P(None, "col", None, None, None),
            P("row", "col", None),
            P("row", "col", None, None),
            P("row", "col", None, None, None),
            P("row", "col", None, None, None),
            P("row", "col"),
        ),
        out_specs=P("row", "col", None, None, None),
        check_vma=False,
    )
```

```python
import functools

import jax
import jax.numpy as jnp
from jax import lax
from jax.experimental import pallas as pl
from jax.experimental.pallas import tpu as pltpu
from jax.sharding import PartitionSpec as P

ABSORB = 3
CHUNKS = 8
LEFT_PARTS = 4
MESH = pl.DeviceIdType.MESH
BF16 = jnp.bfloat16
F32 = jnp.float32


def dot(a, b):
    return lax.dot_general(a, b, (((1,), (0,)), ((), ())), preferred_element_type=F32)


def dot_t(a, b):
    return lax.dot_general(a, b, (((1,), (1,)), ((), ())), preferred_element_type=F32)


def iota(shape, dim):
    return lax.broadcasted_iota(jnp.int32, shape, dim)


def block_operator(tensor_ref, charges_ref, inner, group):
    wide = inner * inner * inner
    row = iota((inner, wide), 0)
    col = iota((inner, wide), 1)
    up, down, right = col // (inner * inner), (col // inner) % inner, col % inner
    flat = tensor_ref[...].astype(F32)
    value = jnp.zeros((inner, wide), F32)
    total = jnp.zeros((inner, wide), jnp.int32)
    for v in range(inner):
        value = jnp.where(row == v, flat[:, v * wide : (v + 1) * wide], value)
        total = total + jnp.where(row == v, charges_ref[0, v], 0)
        total = total + jnp.where(up == v, charges_ref[1, v], 0)
        total = total - jnp.where(down == v, charges_ref[2, v], 0)
        total = total - jnp.where(right == v, charges_ref[3, v], 0)
    total = total + 6
    value = jnp.where(total % 3 == 0, value, 0.0)
    block = inner * group
    full = inner * block
    tiled = jnp.concatenate([value] * (full // inner), axis=0)
    down_of_row = iota((full, wide), 0) // block
    down_of_col = (iota((full, wide), 1) // inner) % inner
    tiled = jnp.where(down_of_row == down_of_col, tiled, 0.0).astype(BF16)
    src, dst = iota((wide, full), 0), iota((wide, full), 1)
    same_up = src // (inner * inner) == dst % inner
    same_right = src % inner == dst // block
    pick = jnp.where(same_up & same_right, 1.0, 0.0).astype(BF16)
    spread = dot(tiled, pick)
    a_row = (iota((full, full), 0) // inner) % group
    a_col = (iota((full, full), 1) // inner) % group
    return jnp.where(a_row == a_col, spread, 0.0)


def kernel(
    outer,
    inner,
    envs,
    start_ref,
    kept_ref,
    charges_ref,
    tensor_hbm,
    initial_hbm,
    right_hbm,
    left_hbm,
    out_ref,
    tensor_ref,
    initial_v,
    chosen,
    raw,
    right_v,
    left_own,
    left_in,
    half,
    sites,
    acc,
    operator,
    outgoing,
    arrived,
    load_sem,
    initial_sem,
    left_send,
    left_recv,
    send_sem,
    recv_sem,
    passing,
    relay_send,
    relay_recv,
):
    rows, cols = lax.axis_size("row"), lax.axis_size("col")
    row, col = lax.axis_index("row"), lax.axis_index("col")
    right_col = lax.rem(col + 1, cols)
    left_col = lax.rem(col + cols - 1, cols)
    size = outer * inner
    part = size // CHUNKS
    keys = outer // CHUNKS
    full = outer
    lanes = full // 2
    group = full // (inner * inner)
    block = group * inner
    pairs = inner // 2

    def working(step):
        return (row >= step) & (row <= rows - ABSORB + step)

    cross = rows // 2 - 1
    crosses = row == cross
    relays = row == rows - 1
    lands = row == cross + 1
    far_col = lax.rem(col + cols // 2, cols)
    sends_any = row < rows - 1
    receives_any = row > 0
    odd = lax.rem(col, 2) == 1

    load_left = pltpu.make_async_copy(left_hbm, raw.at[0], load_sem.at[0])
    load_right = pltpu.make_async_copy(right_hbm, raw.at[1], load_sem.at[1])
    load_tensor = pltpu.make_async_copy(tensor_hbm, tensor_ref, load_sem.at[2])
    load_tensor.start()
    load_left.start()
    load_right.start()

    def load_initial(i):
        span = pl.ds(i * 4 * part, 4 * part)
        return pltpu.make_async_copy(initial_hbm.at[:, span, :], initial_v.at[:, span, :], initial_sem.at[i])

    load_initial(0).start()

    barrier = pltpu.get_barrier_semaphore()
    pl.semaphore_signal(barrier, inc=1, device_id=(row, left_col), device_id_type=MESH)

    @pl.when(receives_any)
    def _():
        pl.semaphore_signal(barrier, inc=1, device_id=(row - 1, col), device_id_type=MESH)

    @pl.when(relays)
    def _():
        pl.semaphore_signal(barrier, inc=1, device_id=(cross, far_col), device_id_type=MESH)

    @pl.when(lands)
    def _():
        pl.semaphore_signal(barrier, inc=1, device_id=(rows - 1, far_col), device_id_type=MESH)

    kept = kept_ref[0, 0]
    load_tensor.wait()
    operator[...] = block_operator(tensor_ref, charges_ref, inner, group).astype(BF16)

    load_left.wait()
    load_initial(1).start()
    to, frm = iota((full, full), 0), iota((full, full), 1)
    keep_eye = jnp.where((to == frm) & (to < kept), 1.0, 0.0).astype(BF16)
    for i in range(CHUNKS):
        left_own[:, i * part : (i + 1) * part] = dot_t(keep_eye, raw[0, i * part : (i + 1) * part, :]).astype(BF16)

    def left_copy(i):
        span = pl.ds(i * (outer // LEFT_PARTS), outer // LEFT_PARTS)
        return pltpu.make_async_remote_copy(
            src_ref=left_own.at[span, :],
            dst_ref=left_in.at[span, :],
            send_sem=left_send.at[i],
            recv_sem=left_recv.at[i],
            device_id=(row, right_col),
            device_id_type=MESH,
        )

    pl.semaphore_wait(barrier, 1 + jnp.where(sends_any, 1, 0) + jnp.where(crosses, 1, 0) + jnp.where(relays, 1, 0))
    for i in range(LEFT_PARTS):
        left_copy(i).start()

    def boundary_copy(step, h, i):
        span = pl.ds(i * part, part)
        return pltpu.make_async_remote_copy(
            src_ref=outgoing.at[step, h, span, :],
            dst_ref=arrived.at[step, h, span, :],
            send_sem=send_sem.at[step, h, i],
            recv_sem=recv_sem.at[step, h, i],
            device_id=(row + 1, col),
            device_id_type=MESH,
        )

    def to_relay(step, i):
        span = pl.ds(i * part, part)
        return pltpu.make_async_remote_copy(
            src_ref=outgoing.at[step, 1, span, :],
            dst_ref=passing.at[step, span, :],
            send_sem=send_sem.at[step, 1, i],
            recv_sem=relay_recv.at[step, i],
            device_id=(rows - 1, far_col),
            device_id_type=MESH,
        )

    def from_relay(step, i):
        span = pl.ds(i * part, part)
        return pltpu.make_async_remote_copy(
            src_ref=passing.at[step, span, :],
            dst_ref=arrived.at[step, 1, span, :],
            send_sem=relay_send.at[step, i],
            recv_sem=recv_sem.at[step, 1, i],
            device_id=(cross + 1, far_col),
            device_id_type=MESH,
        )

    def pass_on(step, i):
        to_relay(step, i).wait_recv()
        from_relay(step, i).start()

    def give(step, h, i):
        if h == 0:
            boundary_copy(step, 0, i).start()
        else:

            @pl.when(crosses)
            def _():
                to_relay(step, i).start()

            @pl.when(jnp.logical_not(crosses))
            def _():
                boundary_copy(step, 1, i).start()

    load_right.wait()
    split = jnp.where(frm == (to % keys) * inner + to // keys, 1.0, 0.0).astype(BF16)
    merge = jnp.where(frm == (to % inner) * keys + to // inner, 1.0, 0.0).astype(BF16)
    inside = frm < kept
    for i in range(CHUNKS):
        moved = dot(split, raw[1, i * part : (i + 1) * part, :])
        moved = jnp.where(inside, moved, 0.0).astype(BF16)
        for s in range(inner):
            for h in range(2):
                right_v[h, s // 2, i * keys : (i + 1) * keys, (s % 2) * lanes : (s % 2 + 1) * lanes] = moved[
                    s * keys : (s + 1) * keys, h * lanes : (h + 1) * lanes
                ]

    def absorb_sites(x, h, at):
        count = x.shape[0]
        for p in range(pairs):
            y = dot(x, right_v[h, p]).astype(BF16)
            half[h, 2 * p, :count] = y[:, :lanes]
            half[h, 2 * p + 1, :count] = y[:, lanes:]
        for g in range(0, count // block, 2):
            sides = [half[h, :, (g + n) * block : (g + n + 1) * block, :].reshape(full, lanes) for n in range(2)]
            y = dot(operator[...], jnp.concatenate(sides, axis=1)).astype(BF16)
            for d in range(inner):
                for n in range(2):
                    sites[h, d // 2, pl.ds(at + (g + n) * block, block), (d % 2) * lanes : (d % 2 + 1) * lanes] = y[
                        d * block : (d + 1) * block, n * lanes : (n + 1) * lanes
                    ]

    def merged(halves, i):
        span = pl.ds(i * keys, keys)
        sides = []
        for h in halves:
            stacked = [acc[h, d // 2, span, (d % 2) * lanes : (d % 2 + 1) * lanes] for d in range(inner)]
            sides.append(jnp.concatenate(stacked, axis=0).astype(BF16))
        return dot(merge, jnp.concatenate(sides, axis=1)).astype(BF16)

    flags = [jnp.where(start_ref[e] == row, 1.0, 0.0) for e in range(envs)]

    def choose(i, carry):
        load_initial(i).wait()

        at = pl.multiple_of(i * 4 * part, 4 * part)
        span = pl.ds(at, 4 * part)
        x = initial_v[0, span, :] * jnp.full((4 * part, outer), flags[0], F32).astype(BF16)
        for e in range(1, envs):
            x = x + initial_v[e, span, :] * jnp.full((4 * part, outer), flags[e], F32).astype(BF16)
        chosen[span, :] = x
        absorb_sites(x, 0, at)
        return carry

    lax.fori_loop(0, CHUNKS // 4, choose, 0)

    def give_first(h, lo=0, hi=CHUNKS):
        span = pl.ds(lo * keys, (hi - lo) * keys)
        for p in range(pairs):
            acc[h, p, span, :] = dot(left_in[span, :], sites[h, p])
        for i in range(lo, hi):
            outgoing[0, h, i * part : (i + 1) * part, :] = merged((h,), i)

            @pl.when(working(0))
            def _(i=i):
                give(0, h, i)

    def second(i, carry):
        at = pl.multiple_of(i * 4 * part, 4 * part)
        absorb_sites(chosen[pl.ds(at, 4 * part), :], 1, at)
        return carry

    late = lax.rem(col, cols // 2) == 0

    @pl.when(odd)
    def _():
        for i in range(LEFT_PARTS):
            left_copy(i).wait_recv()
        give_first(0)
        lax.fori_loop(0, CHUNKS // 4, second, 0)
        give_first(1)

    @pl.when(jnp.logical_not(odd))
    def _():
        lax.fori_loop(0, CHUNKS // 4, second, 0)

    @pl.when(jnp.logical_not(odd | late))
    def _():
        for i in range(LEFT_PARTS):
            left_copy(i).wait_recv()
        for h in range(2):
            give_first(h)

    @pl.when(late)
    def _():
        for n in range(2):
            for i in range(LEFT_PARTS // 2):
                left_copy(n * LEFT_PARTS // 2 + i).wait_recv()
            for h in range(2):
                give_first(h, n * CHUNKS // 2, (n + 1) * CHUNKS // 2)

    @pl.when(relays)
    def _():
        for i in range(CHUNKS):
            pass_on(0, i)

    def later(step):
        def take(i, carry, count=2, last=False):
            for n in range(count):
                for h in range(2):
                    boundary_copy(step - 1, h, i * count + n).wait_recv()

            at = pl.multiple_of(i * count * part, count * part)
            span = pl.ds(at, count * part)
            x = jnp.concatenate([arrived[step - 1, h, span, :] for h in range(2)], axis=1)
            for h in range(2):
                absorb_sites(x, h, at)
            for h in range(2):
                for p in range(pairs):
                    total = acc[h, p] + dot(left_in[:, span], sites[h, p, span, :])
                    if last:
                        for n in range(2):
                            out_ref[2 * p + n, :, h * lanes : (h + 1) * lanes] = total[:, n * lanes : (n + 1) * lanes].astype(BF16)
                    else:
                        acc[h, p] = total
            return carry

        if step == ABSORB - 1:

            @pl.when(relays)
            def _():
                for i in range(CHUNKS):
                    pass_on(step - 1, i)

        acc[...] = jnp.zeros_like(acc)
        lax.fori_loop(0, CHUNKS // 2 - 1, take, 0)
        if step < ABSORB - 1:
            lax.fori_loop(CHUNKS - 2, CHUNKS, functools.partial(take, count=1), 0)
        else:
            lax.fori_loop(CHUNKS - 2, CHUNKS - 1, functools.partial(take, count=1), 0)
            take(CHUNKS - 1, 0, count=1, last=True)
            return

        for i in range(CHUNKS):
            made = merged((0, 1), i)
            for h in range(2):
                outgoing[step, h, i * part : (i + 1) * part, :] = made[:, h * lanes : (h + 1) * lanes]
                give(step, h, i)

    for step in range(1, ABSORB):

        @pl.when(working(step))
        def _(step=step):
            later(step)

    @pl.when(jnp.logical_not(working(ABSORB - 1)))
    def _():
        out_ref[...] = jnp.zeros_like(out_ref)

    for i in range(LEFT_PARTS):
        left_copy(i).wait_send()

    for step in range(ABSORB - 1):

        @pl.when(working(step))
        def _(step=step):
            for h in range(2):
                for i in range(CHUNKS):
                    boundary_copy(step, h, i).wait_send()

        @pl.when(relays)
        def _(step=step):
            for i in range(CHUNKS):
                from_relay(step, i).wait_send()


def shards(start_rows, initial, site_tensors, charges, right_proj, left_proj, kept_ranks):
    envs, _, outer, inner, _ = initial.shape
    size = outer * inner
    smem = pl.BlockSpec(memory_space=pltpu.SMEM)
    vmem = pl.BlockSpec(memory_space=pltpu.VMEM)
    hbm = pl.BlockSpec(memory_space=pltpu.HBM)
    out = pl.pallas_call(
        functools.partial(kernel, outer, inner, envs),
        out_shape=pltpu.VMEM((inner, outer, outer), BF16),
        in_specs=[smem, smem, smem, hbm, hbm, hbm, hbm],
        out_specs=vmem,
        scratch_shapes=[
            pltpu.VMEM((1, inner**4), BF16),
            pltpu.VMEM((envs, size, outer), BF16),
            pltpu.VMEM((size, outer), BF16),
            pltpu.VMEM((2, size, outer), BF16),
            pltpu.VMEM((2, inner // 2, outer, outer), BF16),
            pltpu.VMEM((outer, size), BF16),
            pltpu.VMEM((outer, size), BF16),
            pltpu.VMEM((2, inner, 4 * size // CHUNKS, outer // 2), BF16),
            pltpu.VMEM((2, inner // 2, size, outer), BF16),
            pltpu.VMEM((2, inner // 2, outer, outer), F32),
            pltpu.VMEM((outer, outer), BF16),
            pltpu.VMEM((ABSORB - 1, 2, size, outer // 2), BF16),
            pltpu.VMEM((ABSORB - 1, 2, size, outer // 2), BF16),
            pltpu.SemaphoreType.DMA((3,)),
            pltpu.SemaphoreType.DMA((CHUNKS // 4,)),
            pltpu.SemaphoreType.DMA((LEFT_PARTS,)),
            pltpu.SemaphoreType.DMA((LEFT_PARTS,)),
            pltpu.SemaphoreType.DMA((ABSORB - 1, 2, CHUNKS)),
            pltpu.SemaphoreType.DMA((ABSORB - 1, 2, CHUNKS)),
            pltpu.VMEM((ABSORB - 1, size, outer // 2), BF16),
            pltpu.SemaphoreType.DMA((ABSORB - 1, CHUNKS)),
            pltpu.SemaphoreType.DMA((ABSORB - 1, CHUNKS)),
        ],
        compiler_params=pltpu.CompilerParams(
            collective_id=0, has_side_effects=True, vmem_limit_bytes=58 * 1024 * 1024
        ),
        cost_estimate=pl.CostEstimate(
            flops=ABSORB * 6 * size * size * outer, bytes_accessed=8 * size * outer * 2, transcendentals=0
        ),
    )(
        start_rows,
        kept_ranks,
        charges[0, 0],
        site_tensors[0],
        initial.reshape(envs, size, outer),
        right_proj.reshape(size, outer),
        left_proj.reshape(size, outer),
    )
    return out.transpose(1, 0, 2)[None, None]


def solution(mesh):
    return jax.shard_map(
        shards,
        mesh=mesh,
        in_specs=(
            P(),
            P(None, "col", None, None, None),
            P("row", "col", None),
            P("row", "col", None, None),
            P("row", "col", None, None, None),
            P("row", "col", None, None, None),
            P("row", "col"),
        ),
        out_specs=P("row", "col", None, None, None),
        check_vma=False,
    )
```

```python
import functools

import jax
import jax.numpy as jnp
from jax import lax
from jax.experimental import pallas as pl
from jax.experimental.pallas import tpu as pltpu
from jax.sharding import PartitionSpec as P

ABSORB = 3
CHUNKS = 8
LEFT_PARTS = 4
MESH = pl.DeviceIdType.MESH
BF16 = jnp.bfloat16
F32 = jnp.float32


def dot(a, b):
    return lax.dot_general(a, b, (((1,), (0,)), ((), ())), preferred_element_type=F32)


def dot_t(a, b):
    return lax.dot_general(a, b, (((1,), (1,)), ((), ())), preferred_element_type=F32)


def iota(shape, dim):
    return lax.broadcasted_iota(jnp.int32, shape, dim)


def block_operator(tensor_ref, charges_ref, inner, group):
    wide = inner * inner * inner
    row = iota((inner, wide), 0)
    col = iota((inner, wide), 1)
    up, down, right = col // (inner * inner), (col // inner) % inner, col % inner
    flat = tensor_ref[...].astype(F32)
    value = jnp.zeros((inner, wide), F32)
    total = jnp.zeros((inner, wide), jnp.int32)
    for v in range(inner):
        value = jnp.where(row == v, flat[:, v * wide : (v + 1) * wide], value)
        total = total + jnp.where(row == v, charges_ref[0, v], 0)
        total = total + jnp.where(up == v, charges_ref[1, v], 0)
        total = total - jnp.where(down == v, charges_ref[2, v], 0)
        total = total - jnp.where(right == v, charges_ref[3, v], 0)
    total = total + 6
    value = jnp.where(total % 3 == 0, value, 0.0)
    block = inner * group
    full = inner * block
    tiled = jnp.concatenate([value] * (full // inner), axis=0)
    down_of_row = iota((full, wide), 0) // block
    down_of_col = (iota((full, wide), 1) // inner) % inner
    tiled = jnp.where(down_of_row == down_of_col, tiled, 0.0).astype(BF16)
    src, dst = iota((wide, full), 0), iota((wide, full), 1)
    same_up = src // (inner * inner) == dst % inner
    same_right = src % inner == dst // block
    pick = jnp.where(same_up & same_right, 1.0, 0.0).astype(BF16)
    spread = dot(tiled, pick)
    a_row = (iota((full, full), 0) // inner) % group
    a_col = (iota((full, full), 1) // inner) % group
    return jnp.where(a_row == a_col, spread, 0.0)


def kernel(
    outer,
    inner,
    envs,
    start_ref,
    kept_ref,
    charges_ref,
    tensor_hbm,
    initial_hbm,
    right_hbm,
    left_hbm,
    out_ref,
    tensor_ref,
    initial_v,
    chosen,
    raw,
    right_v,
    left_own,
    left_in,
    half,
    sites,
    acc,
    operator,
    outgoing,
    arrived,
    load_sem,
    initial_sem,
    left_send,
    left_recv,
    send_sem,
    recv_sem,
    passing,
    relay_send,
    relay_recv,
    turn,
):
    rows, cols = lax.axis_size("row"), lax.axis_size("col")
    row, col = lax.axis_index("row"), lax.axis_index("col")
    right_col = lax.rem(col + 1, cols)
    left_col = lax.rem(col + cols - 1, cols)
    size = outer * inner
    part = size // CHUNKS
    keys = outer // CHUNKS
    full = outer
    lanes = full // 2
    group = full // (inner * inner)
    block = group * inner
    pairs = inner // 2

    def working(step):
        return (row >= step) & (row <= rows - ABSORB + step)

    turn_rows = rows // 2
    cross = turn_rows - 1
    lands = row == cross + 1
    crosses = (row == cross) | lands
    relays = (row == rows - 1) | (row == 0)
    behind_relay = (row == cross + 1) | (row == cross + 2)
    opposite = lax.rem(row + turn_rows, rows)
    far_col = lax.rem(col + cols // 2, cols)
    sends_any = row < rows - 1
    receives_any = row > 0
    odd = lax.rem(col, 2) == 1

    load_left = pltpu.make_async_copy(left_hbm, raw.at[0], load_sem.at[0])
    load_right = pltpu.make_async_copy(right_hbm, raw.at[1], load_sem.at[1])
    load_tensor = pltpu.make_async_copy(tensor_hbm, tensor_ref, load_sem.at[2])
    load_tensor.start()
    load_left.start()
    load_right.start()

    def load_initial(i):
        span = pl.ds(i * 4 * part, 4 * part)
        return pltpu.make_async_copy(initial_hbm.at[:, span, :], initial_v.at[:, span, :], initial_sem.at[i])

    load_initial(0).start()

    barrier = pltpu.get_barrier_semaphore()
    pl.semaphore_signal(barrier, inc=1, device_id=(row, left_col), device_id_type=MESH)

    @pl.when(receives_any)
    def _():
        pl.semaphore_signal(barrier, inc=1, device_id=(row - 1, col), device_id_type=MESH)

    @pl.when(relays)
    def _():
        pl.semaphore_signal(barrier, inc=1, device_id=(opposite, far_col), device_id_type=MESH)

    @pl.when(behind_relay)
    def _():
        before = lax.rem(row + turn_rows - 1, rows)
        pl.semaphore_signal(barrier, inc=1, device_id=(before, far_col), device_id_type=MESH)

    kept = kept_ref[0, 0]
    load_tensor.wait()
    operator[...] = block_operator(tensor_ref, charges_ref, inner, group).astype(BF16)

    load_left.wait()
    load_initial(1).start()
    to, frm = iota((full, full), 0), iota((full, full), 1)
    keep_eye = jnp.where((to == frm) & (to < kept), 1.0, 0.0).astype(BF16)
    for i in range(CHUNKS):
        left_own[:, i * part : (i + 1) * part] = dot_t(keep_eye, raw[0, i * part : (i + 1) * part, :]).astype(BF16)

    def left_copy(i):
        span = pl.ds(i * (outer // LEFT_PARTS), outer // LEFT_PARTS)
        return pltpu.make_async_remote_copy(
            src_ref=left_own.at[span, :],
            dst_ref=left_in.at[span, :],
            send_sem=left_send.at[i],
            recv_sem=left_recv.at[i],
            device_id=(row, right_col),
            device_id_type=MESH,
        )

    pl.semaphore_wait(barrier, 1 + jnp.where(sends_any, 1, 0) + jnp.where(crosses, 1, 0) + jnp.where(relays, 1, 0))
    for i in range(LEFT_PARTS):
        left_copy(i).start()

    def boundary_copy(step, h, i):
        span = pl.ds(i * part, part)
        return pltpu.make_async_remote_copy(
            src_ref=outgoing.at[step, h, span, :],
            dst_ref=arrived.at[step, h, span, :],
            send_sem=send_sem.at[step, h, i],
            recv_sem=recv_sem.at[step, h, i],
            device_id=(row + 1, col),
            device_id_type=MESH,
        )

    def to_relay(step, i):
        span = pl.ds(i * part, part)
        return pltpu.make_async_remote_copy(
            src_ref=outgoing.at[step, 1, span, :],
            dst_ref=passing.at[step, span, :],
            send_sem=send_sem.at[step, 1, i],
            recv_sem=relay_recv.at[step, i],
            device_id=(opposite, far_col),
            device_id_type=MESH,
        )

    def from_relay(step, i):
        span = pl.ds(i * part, part)
        return pltpu.make_async_remote_copy(
            src_ref=passing.at[step, span, :],
            dst_ref=arrived.at[step, 1, span, :],
            send_sem=relay_send.at[step, i],
            recv_sem=recv_sem.at[step, 1, i],
            device_id=(lax.rem(row + turn_rows + 1, rows), far_col),
            device_id_type=MESH,
        )

    def pass_on(step, i):
        to_relay(step, i).wait_recv()
        from_relay(step, i).start()

    def relayed(step):
        shared = lax.rem(col, cols // 2) < 2
        main = (row == cross) | (row == rows - 1)
        return main | shared if step > 0 else main & shared

    def give(step, h, i):
        if h == 0:
            boundary_copy(step, 0, i).start()
        else:
            around = crosses & relayed(step)

            @pl.when(around)
            def _():
                to_relay(step, i).start()

            @pl.when(jnp.logical_not(around))
            def _():
                boundary_copy(step, 1, i).start()

    load_right.wait()
    split = jnp.where(frm == (to % keys) * inner + to // keys, 1.0, 0.0).astype(BF16)
    merge = jnp.where(frm == (to % inner) * keys + to // inner, 1.0, 0.0).astype(BF16)
    inside = frm < kept
    for i in range(CHUNKS):
        moved = dot(split, raw[1, i * part : (i + 1) * part, :])
        moved = jnp.where(inside, moved, 0.0).astype(BF16)
        for s in range(inner):
            for h in range(2):
                right_v[h, s // 2, i * keys : (i + 1) * keys, (s % 2) * lanes : (s % 2 + 1) * lanes] = moved[
                    s * keys : (s + 1) * keys, h * lanes : (h + 1) * lanes
                ]

    def absorb_sites(x, h, at):
        count = x.shape[0]
        for p in range(pairs):
            y = dot(x, right_v[h, p]).astype(BF16)
            half[h, 2 * p, :count] = y[:, :lanes]
            half[h, 2 * p + 1, :count] = y[:, lanes:]
        for g in range(0, count // block, 2):
            sides = [half[h, :, (g + n) * block : (g + n + 1) * block, :].reshape(full, lanes) for n in range(2)]
            y = dot(operator[...], jnp.concatenate(sides, axis=1)).astype(BF16)
            for d in range(inner):
                for n in range(2):
                    sites[h, d // 2, pl.ds(at + (g + n) * block, block), (d % 2) * lanes : (d % 2 + 1) * lanes] = y[
                        d * block : (d + 1) * block, n * lanes : (n + 1) * lanes
                    ]

    def merged(halves, i):
        span = pl.ds(i * keys, keys)
        sides = []
        for h in halves:
            stacked = [acc[h, d // 2, span, (d % 2) * lanes : (d % 2 + 1) * lanes] for d in range(inner)]
            sides.append(jnp.concatenate(stacked, axis=0).astype(BF16))
        return dot(merge, jnp.concatenate(sides, axis=1)).astype(BF16)

    flags = [jnp.where(start_ref[e] == row, 1.0, 0.0) for e in range(envs)]

    def choose(i, carry):
        load_initial(i).wait()

        at = pl.multiple_of(i * 4 * part, 4 * part)
        span = pl.ds(at, 4 * part)
        x = initial_v[0, span, :] * jnp.full((4 * part, outer), flags[0], F32).astype(BF16)
        for e in range(1, envs):
            x = x + initial_v[e, span, :] * jnp.full((4 * part, outer), flags[e], F32).astype(BF16)
        chosen[span, :] = x
        absorb_sites(x, 0, at)
        return carry

    lax.fori_loop(0, CHUNKS // 4, choose, 0)

    def give_first(h, lo=0, hi=CHUNKS):
        span = pl.ds(lo * keys, (hi - lo) * keys)
        for p in range(pairs):
            acc[h, p, span, :] = dot(left_in[span, :], sites[h, p])
        for i in range(lo, hi):
            outgoing[0, h, i * part : (i + 1) * part, :] = merged((h,), i)

            @pl.when(working(0))
            def _(i=i):
                give(0, h, i)

    def second(i, carry):
        at = pl.multiple_of(i * 4 * part, 4 * part)
        absorb_sites(chosen[pl.ds(at, 4 * part), :], 1, at)
        return carry

    late = lax.rem(col, cols // 2) == 0

    @pl.when(odd)
    def _():
        for i in range(LEFT_PARTS):
            left_copy(i).wait_recv()
        give_first(0)
        lax.fori_loop(0, CHUNKS // 4, second, 0)
        give_first(1)

    @pl.when(jnp.logical_not(odd))
    def _():
        lax.fori_loop(0, CHUNKS // 4, second, 0)

    @pl.when(jnp.logical_not(odd | late))
    def _():
        for i in range(LEFT_PARTS):
            left_copy(i).wait_recv()
        for h in range(2):
            give_first(h)

    @pl.when(late)
    def _():
        for n in range(2):
            for i in range(LEFT_PARTS // 2):
                left_copy(n * LEFT_PARTS // 2 + i).wait_recv()
            for h in range(2):
                give_first(h, n * CHUNKS // 2, (n + 1) * CHUNKS // 2)

    @pl.when(relays & relayed(0))
    def _():
        for i in range(CHUNKS):
            pass_on(0, i)

    @pl.when(relays & relayed(1))
    def _():
        for i in range(CHUNKS):
            pass_on(1, i)

    in_turn = jnp.logical_not(lands)

    def later(step):
        def take(i, carry, count=2, last=False):
            for n in range(count):
                for h in range(2):
                    boundary_copy(step - 1, h, i * count + n).wait_recv()

            if step < ABSORB - 1 and count == 2:
                @pl.when(in_turn & jnp.logical_not(odd) & (i == 1))
                def _():
                    pl.semaphore_signal(turn, inc=1, device_id=(row, right_col), device_id_type=MESH)

            at = pl.multiple_of(i * count * part, count * part)
            span = pl.ds(at, count * part)
            x = jnp.concatenate([arrived[step - 1, h, span, :] for h in range(2)], axis=1)
            for h in range(2):
                absorb_sites(x, h, at)
            for h in range(2):
                for p in range(pairs):
                    total = acc[h, p] + dot(left_in[:, span], sites[h, p, span, :])
                    if last:
                        for n in range(2):
                            out_ref[2 * p + n, :, h * lanes : (h + 1) * lanes] = total[:, n * lanes : (n + 1) * lanes].astype(BF16)
                    else:
                        acc[h, p] = total
            return carry

        acc[...] = jnp.zeros_like(acc)
        lax.fori_loop(0, CHUNKS // 2 - 1, take, 0)
        if step < ABSORB - 1:
            lax.fori_loop(CHUNKS - 2, CHUNKS, functools.partial(take, count=1), 0)
        else:
            lax.fori_loop(CHUNKS - 2, CHUNKS - 1, functools.partial(take, count=1), 0)
            take(CHUNKS - 1, 0, count=1, last=True)
            return

        @pl.when(in_turn & odd)
        def _():
            pl.semaphore_wait(turn, 1)

        for i in range(CHUNKS):
            made = merged((0, 1), i)
            for h in range(2):
                outgoing[step, h, i * part : (i + 1) * part, :] = made[:, h * lanes : (h + 1) * lanes]
                give(step, h, i)

    for step in range(1, ABSORB):

        @pl.when(working(step))
        def _(step=step):
            later(step)

    @pl.when(jnp.logical_not(working(ABSORB - 1)))
    def _():
        out_ref[...] = jnp.zeros_like(out_ref)

    for i in range(LEFT_PARTS):
        left_copy(i).wait_send()

    for step in range(ABSORB - 1):

        @pl.when(working(step))
        def _(step=step):
            for h in range(2):
                for i in range(CHUNKS):
                    boundary_copy(step, h, i).wait_send()

        @pl.when(relays & relayed(step))
        def _(step=step):
            for i in range(CHUNKS):
                from_relay(step, i).wait_send()


def shards(start_rows, initial, site_tensors, charges, right_proj, left_proj, kept_ranks):
    envs, _, outer, inner, _ = initial.shape
    size = outer * inner
    smem = pl.BlockSpec(memory_space=pltpu.SMEM)
    vmem = pl.BlockSpec(memory_space=pltpu.VMEM)
    hbm = pl.BlockSpec(memory_space=pltpu.HBM)
    out = pl.pallas_call(
        functools.partial(kernel, outer, inner, envs),
        out_shape=pltpu.VMEM((inner, outer, outer), BF16),
        in_specs=[smem, smem, smem, hbm, hbm, hbm, hbm],
        out_specs=vmem,
        scratch_shapes=[
            pltpu.VMEM((1, inner**4), BF16),
            pltpu.VMEM((envs, size, outer), BF16),
            pltpu.VMEM((size, outer), BF16),
            pltpu.VMEM((2, size, outer), BF16),
            pltpu.VMEM((2, inner // 2, outer, outer), BF16),
            pltpu.VMEM((outer, size), BF16),
            pltpu.VMEM((outer, size), BF16),
            pltpu.VMEM((2, inner, 4 * size // CHUNKS, outer // 2), BF16),
            pltpu.VMEM((2, inner // 2, size, outer), BF16),
            pltpu.VMEM((2, inner // 2, outer, outer), F32),
            pltpu.VMEM((outer, outer), BF16),
            pltpu.VMEM((ABSORB - 1, 2, size, outer // 2), BF16),
            pltpu.VMEM((ABSORB - 1, 2, size, outer // 2), BF16),
            pltpu.SemaphoreType.DMA((3,)),
            pltpu.SemaphoreType.DMA((CHUNKS // 4,)),
            pltpu.SemaphoreType.DMA((LEFT_PARTS,)),
            pltpu.SemaphoreType.DMA((LEFT_PARTS,)),
            pltpu.SemaphoreType.DMA((ABSORB - 1, 2, CHUNKS)),
            pltpu.SemaphoreType.DMA((ABSORB - 1, 2, CHUNKS)),
            pltpu.VMEM((ABSORB - 1, size, outer // 2), BF16),
            pltpu.SemaphoreType.DMA((ABSORB - 1, CHUNKS)),
            pltpu.SemaphoreType.DMA((ABSORB - 1, CHUNKS)),
            pltpu.SemaphoreType.REGULAR,
        ],
        compiler_params=pltpu.CompilerParams(
            collective_id=0, has_side_effects=True, vmem_limit_bytes=58 * 1024 * 1024
        ),
        cost_estimate=pl.CostEstimate(
            flops=ABSORB * 6 * size * size * outer, bytes_accessed=8 * size * outer * 2, transcendentals=0
        ),
    )(
        start_rows,
        kept_ranks,
        charges[0, 0],
        site_tensors[0],
        initial.reshape(envs, size, outer),
        right_proj.reshape(size, outer),
        left_proj.reshape(size, outer),
    )
    return out.transpose(1, 0, 2)[None, None]


def solution(mesh):
    return jax.shard_map(
        shards,
        mesh=mesh,
        in_specs=(
            P(),
            P(None, "col", None, None, None),
            P("row", "col", None),
            P("row", "col", None, None),
            P("row", "col", None, None, None),
            P("row", "col", None, None, None),
            P("row", "col"),
        ),
        out_specs=P("row", "col", None, None, None),
        check_vma=False,
    )
```

```python
import functools

import jax
import jax.numpy as jnp
from jax import lax
from jax.experimental import pallas as pl
from jax.experimental.pallas import tpu as pltpu
from jax.sharding import PartitionSpec as P

ABSORB = 3
CHUNKS = 8
LEFT_PARTS = 4
MESH = pl.DeviceIdType.MESH
BF16 = jnp.bfloat16
F32 = jnp.float32


def dot(a, b):
    return lax.dot_general(a, b, (((1,), (0,)), ((), ())), preferred_element_type=F32)


def dot_t(a, b):
    return lax.dot_general(a, b, (((1,), (1,)), ((), ())), preferred_element_type=F32)


def iota(shape, dim):
    return lax.broadcasted_iota(jnp.int32, shape, dim)


def block_operator(tensor_ref, charges_ref, inner, group):
    wide = inner * inner * inner
    row = iota((inner, wide), 0)
    col = iota((inner, wide), 1)
    up, down, right = col // (inner * inner), (col // inner) % inner, col % inner
    flat = tensor_ref[...].astype(F32)
    value = jnp.zeros((inner, wide), F32)
    total = jnp.zeros((inner, wide), jnp.int32)
    for v in range(inner):
        value = jnp.where(row == v, flat[:, v * wide : (v + 1) * wide], value)
        total = total + jnp.where(row == v, charges_ref[0, v], 0)
        total = total + jnp.where(up == v, charges_ref[1, v], 0)
        total = total - jnp.where(down == v, charges_ref[2, v], 0)
        total = total - jnp.where(right == v, charges_ref[3, v], 0)
    total = total + 6
    value = jnp.where(total % 3 == 0, value, 0.0)
    block = inner * group
    full = inner * block
    tiled = jnp.concatenate([value] * (full // inner), axis=0)
    down_of_row = iota((full, wide), 0) // block
    down_of_col = (iota((full, wide), 1) // inner) % inner
    tiled = jnp.where(down_of_row == down_of_col, tiled, 0.0).astype(BF16)
    src, dst = iota((wide, full), 0), iota((wide, full), 1)
    same_up = src // (inner * inner) == dst % inner
    same_right = src % inner == dst // block
    pick = jnp.where(same_up & same_right, 1.0, 0.0).astype(BF16)
    spread = dot(tiled, pick)
    a_row = (iota((full, full), 0) // inner) % group
    a_col = (iota((full, full), 1) // inner) % group
    return jnp.where(a_row == a_col, spread, 0.0)


def kernel(
    outer,
    inner,
    envs,
    start_ref,
    kept_ref,
    charges_ref,
    tensor_hbm,
    initial_hbm,
    right_hbm,
    left_hbm,
    out_ref,
    tensor_ref,
    initial_v,
    chosen,
    raw,
    right_v,
    left_own,
    left_in,
    half,
    sites,
    acc,
    operator,
    outgoing,
    arrived,
    load_sem,
    initial_sem,
    left_send,
    left_recv,
    send_sem,
    recv_sem,
    passing,
    relay_send,
    relay_recv,
    turn,
):
    rows, cols = lax.axis_size("row"), lax.axis_size("col")
    row, col = lax.axis_index("row"), lax.axis_index("col")
    right_col = lax.rem(col + 1, cols)
    left_col = lax.rem(col + cols - 1, cols)
    size = outer * inner
    part = size // CHUNKS
    keys = outer // CHUNKS
    full = outer
    lanes = full // 2
    group = full // (inner * inner)
    block = group * inner
    pairs = inner // 2

    def working(step):
        return (row >= step) & (row <= rows - ABSORB + step)

    turn_rows = rows // 2
    cross = turn_rows - 1
    lands = row == cross + 1
    crosses = (row == cross) | lands
    relays = (row == rows - 1) | (row == 0)
    behind_relay = (row == cross + 1) | (row == cross + 2)
    opposite = lax.rem(row + turn_rows, rows)
    far_col = lax.rem(col + cols // 2, cols)
    sends_any = row < rows - 1
    receives_any = row > 0
    odd = lax.rem(col, 2) == 1

    load_left = pltpu.make_async_copy(left_hbm, raw.at[0], load_sem.at[0])
    load_right = pltpu.make_async_copy(right_hbm, raw.at[1], load_sem.at[1])
    load_tensor = pltpu.make_async_copy(tensor_hbm, tensor_ref, load_sem.at[2])
    load_tensor.start()
    load_left.start()
    load_right.start()

    def load_initial(i):
        span = pl.ds(i * 4 * part, 4 * part)
        return pltpu.make_async_copy(initial_hbm.at[:, span, :], initial_v.at[:, span, :], initial_sem.at[i])

    load_initial(0).start()

    barrier = pltpu.get_barrier_semaphore()
    pl.semaphore_signal(barrier, inc=1, device_id=(row, left_col), device_id_type=MESH)

    @pl.when(receives_any)
    def _():
        pl.semaphore_signal(barrier, inc=1, device_id=(row - 1, col), device_id_type=MESH)

    @pl.when(relays)
    def _():
        pl.semaphore_signal(barrier, inc=1, device_id=(opposite, far_col), device_id_type=MESH)

    @pl.when(behind_relay)
    def _():
        before = lax.rem(row + turn_rows - 1, rows)
        pl.semaphore_signal(barrier, inc=1, device_id=(before, far_col), device_id_type=MESH)

    kept = kept_ref[0, 0]
    load_tensor.wait()
    operator[...] = block_operator(tensor_ref, charges_ref, inner, group).astype(BF16)

    load_left.wait()
    load_initial(1).start()
    to, frm = iota((full, full), 0), iota((full, full), 1)
    keep_eye = jnp.where((to == frm) & (to < kept), 1.0, 0.0).astype(BF16)
    for i in range(CHUNKS):
        left_own[:, i * part : (i + 1) * part] = dot_t(keep_eye, raw[0, i * part : (i + 1) * part, :]).astype(BF16)

    def left_copy(i):
        span = pl.ds(i * (outer // LEFT_PARTS), outer // LEFT_PARTS)
        return pltpu.make_async_remote_copy(
            src_ref=left_own.at[span, :],
            dst_ref=left_in.at[span, :],
            send_sem=left_send.at[i],
            recv_sem=left_recv.at[i],
            device_id=(row, right_col),
            device_id_type=MESH,
        )

    pl.semaphore_wait(barrier, 1 + jnp.where(sends_any, 1, 0) + jnp.where(crosses, 1, 0) + jnp.where(relays, 1, 0))
    for i in range(LEFT_PARTS):
        left_copy(i).start()

    def boundary_copy(step, h, i):
        span = pl.ds(i * part, part)
        return pltpu.make_async_remote_copy(
            src_ref=outgoing.at[step, h, span, :],
            dst_ref=arrived.at[step, h, span, :],
            send_sem=send_sem.at[step, h, i],
            recv_sem=recv_sem.at[step, h, i],
            device_id=(row + 1, col),
            device_id_type=MESH,
        )

    def to_relay(step, i):
        span = pl.ds(i * part, part)
        return pltpu.make_async_remote_copy(
            src_ref=outgoing.at[step, 1, span, :],
            dst_ref=passing.at[step, span, :],
            send_sem=send_sem.at[step, 1, i],
            recv_sem=relay_recv.at[step, i],
            device_id=(opposite, far_col),
            device_id_type=MESH,
        )

    def from_relay(step, i):
        span = pl.ds(i * part, part)
        return pltpu.make_async_remote_copy(
            src_ref=passing.at[step, span, :],
            dst_ref=arrived.at[step, 1, span, :],
            send_sem=relay_send.at[step, i],
            recv_sem=recv_sem.at[step, 1, i],
            device_id=(lax.rem(row + turn_rows + 1, rows), far_col),
            device_id_type=MESH,
        )

    def pass_on(step, i):
        to_relay(step, i).wait_recv()
        from_relay(step, i).start()

    def relayed(step):
        shared = lax.rem(col, cols // 2) < 2
        main = (row == cross) | (row == rows - 1)
        return main | shared if step > 0 else main & shared

    def give(step, h, i):
        if h == 0:
            boundary_copy(step, 0, i).start()
        else:
            around = crosses & relayed(step)

            @pl.when(around)
            def _():
                to_relay(step, i).start()

            @pl.when(jnp.logical_not(around))
            def _():
                boundary_copy(step, 1, i).start()

    load_right.wait()
    split = jnp.where(frm == (to % keys) * inner + to // keys, 1.0, 0.0).astype(BF16)
    merge = jnp.where(frm == (to % inner) * keys + to // inner, 1.0, 0.0).astype(BF16)
    inside = frm < kept
    for i in range(CHUNKS):
        moved = dot(split, raw[1, i * part : (i + 1) * part, :])
        moved = jnp.where(inside, moved, 0.0).astype(BF16)
        for s in range(inner):
            for h in range(2):
                right_v[h, s // 2, i * keys : (i + 1) * keys, (s % 2) * lanes : (s % 2 + 1) * lanes] = moved[
                    s * keys : (s + 1) * keys, h * lanes : (h + 1) * lanes
                ]

    def absorb_sites(x, h, at):
        count = x.shape[0]
        for p in range(pairs):
            y = dot(x, right_v[h, p]).astype(BF16)
            half[h, 2 * p, :count] = y[:, :lanes]
            half[h, 2 * p + 1, :count] = y[:, lanes:]
        for g in range(0, count // block, 2):
            sides = [half[h, :, (g + n) * block : (g + n + 1) * block, :].reshape(full, lanes) for n in range(2)]
            y = dot(operator[...], jnp.concatenate(sides, axis=1)).astype(BF16)
            for d in range(inner):
                for n in range(2):
                    sites[h, d // 2, pl.ds(at + (g + n) * block, block), (d % 2) * lanes : (d % 2 + 1) * lanes] = y[
                        d * block : (d + 1) * block, n * lanes : (n + 1) * lanes
                    ]

    def merged(halves, i):
        span = pl.ds(i * keys, keys)
        sides = []
        for h in halves:
            stacked = [acc[h, d // 2, span, (d % 2) * lanes : (d % 2 + 1) * lanes] for d in range(inner)]
            sides.append(jnp.concatenate(stacked, axis=0).astype(BF16))
        return dot(merge, jnp.concatenate(sides, axis=1)).astype(BF16)

    flags = [jnp.where(start_ref[e] == row, 1.0, 0.0) for e in range(envs)]

    def choose(i, carry):
        load_initial(i).wait()

        at = pl.multiple_of(i * 4 * part, 4 * part)
        span = pl.ds(at, 4 * part)
        x = initial_v[0, span, :] * jnp.full((4 * part, outer), flags[0], F32).astype(BF16)
        for e in range(1, envs):
            x = x + initial_v[e, span, :] * jnp.full((4 * part, outer), flags[e], F32).astype(BF16)
        chosen[span, :] = x
        absorb_sites(x, 0, at)
        return carry

    lax.fori_loop(0, CHUNKS // 4, choose, 0)

    def give_first(h, lo=0, hi=CHUNKS):
        span = pl.ds(lo * keys, (hi - lo) * keys)
        for p in range(pairs):
            acc[h, p, span, :] = dot(left_in[span, :], sites[h, p])
        for i in range(lo, hi):
            outgoing[0, h, i * part : (i + 1) * part, :] = merged((h,), i)

            @pl.when(working(0))
            def _(i=i):
                give(0, h, i)

    def second(i, carry):
        at = pl.multiple_of(i * 4 * part, 4 * part)
        absorb_sites(chosen[pl.ds(at, 4 * part), :], 1, at)
        return carry

    late = lax.rem(col, cols // 2) == 0

    @pl.when(odd)
    def _():
        for i in range(LEFT_PARTS):
            left_copy(i).wait_recv()
        give_first(0)
        lax.fori_loop(0, CHUNKS // 4, second, 0)
        give_first(1)

    @pl.when(jnp.logical_not(odd))
    def _():
        lax.fori_loop(0, CHUNKS // 4, second, 0)

    @pl.when(jnp.logical_not(odd | late))
    def _():
        for i in range(LEFT_PARTS):
            left_copy(i).wait_recv()
        for h in range(2):
            give_first(h)

    @pl.when(late)
    def _():
        for n in range(2):
            for i in range(LEFT_PARTS // 2):
                left_copy(n * LEFT_PARTS // 2 + i).wait_recv()
            for h in range(2):
                give_first(h, n * CHUNKS // 2, (n + 1) * CHUNKS // 2)

    @pl.when(relays & relayed(0))
    def _():
        for i in range(CHUNKS):
            pass_on(0, i)

    @pl.when(relays & relayed(1))
    def _():
        for i in range(CHUNKS):
            pass_on(1, i)

    in_turn = jnp.logical_not(lands)

    def later(step):
        def take(i, carry, count=2, last=False):
            for n in range(count):
                for h in range(2):
                    boundary_copy(step - 1, h, i * count + n).wait_recv()

            if step < ABSORB - 1 and count == 2:
                @pl.when(in_turn & jnp.logical_not(odd) & (i == 1))
                def _():
                    pl.semaphore_signal(turn, inc=1, device_id=(row, right_col), device_id_type=MESH)

            at = pl.multiple_of(i * count * part, count * part)
            span = pl.ds(at, count * part)
            x = jnp.concatenate([arrived[step - 1, h, span, :] for h in range(2)], axis=1)
            for h in range(2):
                absorb_sites(x, h, at)
            for h in range(2):
                for p in range(pairs):
                    total = acc[h, p] + dot(left_in[:, span], sites[h, p, span, :])
                    if last:
                        for n in range(2):
                            out_ref[2 * p + n, :, h * lanes : (h + 1) * lanes] = total[:, n * lanes : (n + 1) * lanes].astype(BF16)
                    else:
                        acc[h, p] = total
            return carry

        acc[...] = jnp.zeros_like(acc)
        if step < ABSORB - 1:
            lax.fori_loop(0, CHUNKS // 2 - 1, take, 0)
            lax.fori_loop(CHUNKS - 2, CHUNKS, functools.partial(take, count=1), 0)
        else:
            lax.fori_loop(0, CHUNKS // 2 - 2, take, 0)
            lax.fori_loop(CHUNKS - 4, CHUNKS - 1, functools.partial(take, count=1), 0)
            take(CHUNKS - 1, 0, count=1, last=True)
            return

        @pl.when(in_turn & odd)
        def _():
            pl.semaphore_wait(turn, 1)

        for i in range(CHUNKS):
            made = merged((0, 1), i)
            for h in range(2):
                outgoing[step, h, i * part : (i + 1) * part, :] = made[:, h * lanes : (h + 1) * lanes]
                give(step, h, i)

    for step in range(1, ABSORB):

        @pl.when(working(step))
        def _(step=step):
            later(step)

    @pl.when(jnp.logical_not(working(ABSORB - 1)))
    def _():
        out_ref[...] = jnp.zeros_like(out_ref)

    for i in range(LEFT_PARTS):
        left_copy(i).wait_send()

    for step in range(ABSORB - 1):

        @pl.when(working(step))
        def _(step=step):
            for h in range(2):
                for i in range(CHUNKS):
                    boundary_copy(step, h, i).wait_send()

        @pl.when(relays & relayed(step))
        def _(step=step):
            for i in range(CHUNKS):
                from_relay(step, i).wait_send()


def shards(start_rows, initial, site_tensors, charges, right_proj, left_proj, kept_ranks):
    envs, _, outer, inner, _ = initial.shape
    size = outer * inner
    smem = pl.BlockSpec(memory_space=pltpu.SMEM)
    vmem = pl.BlockSpec(memory_space=pltpu.VMEM)
    hbm = pl.BlockSpec(memory_space=pltpu.HBM)
    out = pl.pallas_call(
        functools.partial(kernel, outer, inner, envs),
        out_shape=pltpu.VMEM((inner, outer, outer), BF16),
        in_specs=[smem, smem, smem, hbm, hbm, hbm, hbm],
        out_specs=vmem,
        scratch_shapes=[
            pltpu.VMEM((1, inner**4), BF16),
            pltpu.VMEM((envs, size, outer), BF16),
            pltpu.VMEM((size, outer), BF16),
            pltpu.VMEM((2, size, outer), BF16),
            pltpu.VMEM((2, inner // 2, outer, outer), BF16),
            pltpu.VMEM((outer, size), BF16),
            pltpu.VMEM((outer, size), BF16),
            pltpu.VMEM((2, inner, 4 * size // CHUNKS, outer // 2), BF16),
            pltpu.VMEM((2, inner // 2, size, outer), BF16),
            pltpu.VMEM((2, inner // 2, outer, outer), F32),
            pltpu.VMEM((outer, outer), BF16),
            pltpu.VMEM((ABSORB - 1, 2, size, outer // 2), BF16),
            pltpu.VMEM((ABSORB - 1, 2, size, outer // 2), BF16),
            pltpu.SemaphoreType.DMA((3,)),
            pltpu.SemaphoreType.DMA((CHUNKS // 4,)),
            pltpu.SemaphoreType.DMA((LEFT_PARTS,)),
            pltpu.SemaphoreType.DMA((LEFT_PARTS,)),
            pltpu.SemaphoreType.DMA((ABSORB - 1, 2, CHUNKS)),
            pltpu.SemaphoreType.DMA((ABSORB - 1, 2, CHUNKS)),
            pltpu.VMEM((ABSORB - 1, size, outer // 2), BF16),
            pltpu.SemaphoreType.DMA((ABSORB - 1, CHUNKS)),
            pltpu.SemaphoreType.DMA((ABSORB - 1, CHUNKS)),
            pltpu.SemaphoreType.REGULAR,
        ],
        compiler_params=pltpu.CompilerParams(
            collective_id=0, has_side_effects=True, vmem_limit_bytes=58 * 1024 * 1024
        ),
        cost_estimate=pl.CostEstimate(
            flops=ABSORB * 6 * size * size * outer, bytes_accessed=8 * size * outer * 2, transcendentals=0
        ),
    )(
        start_rows,
        kept_ranks,
        charges[0, 0],
        site_tensors[0],
        initial.reshape(envs, size, outer),
        right_proj.reshape(size, outer),
        left_proj.reshape(size, outer),
    )
    return out.transpose(1, 0, 2)[None, None]


def solution(mesh):
    return jax.shard_map(
        shards,
        mesh=mesh,
        in_specs=(
            P(),
            P(None, "col", None, None, None),
            P("row", "col", None),
            P("row", "col", None, None),
            P("row", "col", None, None, None),
            P("row", "col", None, None, None),
            P("row", "col"),
        ),
        out_specs=P("row", "col", None, None, None),
        check_vma=False,
    )
```

```python
import functools

import jax
import jax.numpy as jnp
from jax import lax
from jax.experimental import pallas as pl
from jax.experimental.pallas import tpu as pltpu
from jax.sharding import PartitionSpec as P

ABSORB = 3
CHUNKS = 8
LEFT_PARTS = 4
MESH = pl.DeviceIdType.MESH
BF16 = jnp.bfloat16
F32 = jnp.float32


def dot(a, b):
    return lax.dot_general(a, b, (((1,), (0,)), ((), ())), preferred_element_type=F32)


def dot_t(a, b):
    return lax.dot_general(a, b, (((1,), (1,)), ((), ())), preferred_element_type=F32)


def iota(shape, dim):
    return lax.broadcasted_iota(jnp.int32, shape, dim)


def block_operator(tensor_ref, charges_ref, inner, group):
    wide = inner * inner * inner
    row = iota((inner, wide), 0)
    col = iota((inner, wide), 1)
    up, down, right = col // (inner * inner), (col // inner) % inner, col % inner
    flat = tensor_ref[...].astype(F32)
    value = jnp.zeros((inner, wide), F32)
    total = jnp.zeros((inner, wide), jnp.int32)
    for v in range(inner):
        value = jnp.where(row == v, flat[:, v * wide : (v + 1) * wide], value)
        total = total + jnp.where(row == v, charges_ref[0, v], 0)
        total = total + jnp.where(up == v, charges_ref[1, v], 0)
        total = total - jnp.where(down == v, charges_ref[2, v], 0)
        total = total - jnp.where(right == v, charges_ref[3, v], 0)
    total = total + 6
    value = jnp.where(total % 3 == 0, value, 0.0)
    block = inner * group
    full = inner * block
    tiled = jnp.concatenate([value] * (full // inner), axis=0)
    down_of_row = iota((full, wide), 0) // block
    down_of_col = (iota((full, wide), 1) // inner) % inner
    tiled = jnp.where(down_of_row == down_of_col, tiled, 0.0).astype(BF16)
    src, dst = iota((wide, full), 0), iota((wide, full), 1)
    same_up = src // (inner * inner) == dst % inner
    same_right = src % inner == dst // block
    pick = jnp.where(same_up & same_right, 1.0, 0.0).astype(BF16)
    spread = dot(tiled, pick)
    a_row = (iota((full, full), 0) // inner) % group
    a_col = (iota((full, full), 1) // inner) % group
    return jnp.where(a_row == a_col, spread, 0.0)


def kernel(
    outer,
    inner,
    envs,
    start_ref,
    kept_ref,
    charges_ref,
    tensor_hbm,
    initial_hbm,
    right_hbm,
    left_hbm,
    out_ref,
    tensor_ref,
    initial_v,
    chosen,
    raw,
    right_v,
    left_own,
    left_in,
    half,
    sites,
    acc,
    operator,
    outgoing,
    arrived,
    load_sem,
    initial_sem,
    left_send,
    left_recv,
    send_sem,
    recv_sem,
    passing,
    relay_send,
    relay_recv,
    turn,
):
    rows, cols = lax.axis_size("row"), lax.axis_size("col")
    row, col = lax.axis_index("row"), lax.axis_index("col")
    right_col = lax.rem(col + 1, cols)
    left_col = lax.rem(col + cols - 1, cols)
    size = outer * inner
    part = size // CHUNKS
    keys = outer // CHUNKS
    full = outer
    lanes = full // 2
    group = full // (inner * inner)
    block = group * inner
    pairs = inner // 2

    def working(step):
        return (row >= step) & (row <= rows - ABSORB + step)

    turn_rows = rows // 2
    cross = turn_rows - 1
    lands = row == cross + 1
    crosses = (row == cross) | lands
    relays = (row == rows - 1) | (row == 0)
    behind_relay = (row == cross + 1) | (row == cross + 2)
    opposite = lax.rem(row + turn_rows, rows)
    far_col = lax.rem(col + cols // 2, cols)
    sends_any = row < rows - 1
    receives_any = row > 0
    odd = lax.rem(col, 2) == 1

    load_left = pltpu.make_async_copy(left_hbm, raw.at[0], load_sem.at[0])
    load_right = pltpu.make_async_copy(right_hbm, raw.at[1], load_sem.at[1])
    load_tensor = pltpu.make_async_copy(tensor_hbm, tensor_ref, load_sem.at[2])
    load_tensor.start()
    load_left.start()
    load_right.start()

    def load_initial(i):
        span = pl.ds(i * 4 * part, 4 * part)
        return pltpu.make_async_copy(initial_hbm.at[:, span, :], initial_v.at[:, span, :], initial_sem.at[i])

    load_initial(0).start()

    barrier = pltpu.get_barrier_semaphore()
    pl.semaphore_signal(barrier, inc=1, device_id=(row, left_col), device_id_type=MESH)

    @pl.when(receives_any)
    def _():
        pl.semaphore_signal(barrier, inc=1, device_id=(row - 1, col), device_id_type=MESH)

    @pl.when(relays)
    def _():
        pl.semaphore_signal(barrier, inc=1, device_id=(opposite, far_col), device_id_type=MESH)

    @pl.when(behind_relay)
    def _():
        before = lax.rem(row + turn_rows - 1, rows)
        pl.semaphore_signal(barrier, inc=1, device_id=(before, far_col), device_id_type=MESH)

    kept = kept_ref[0, 0]
    load_tensor.wait()
    operator[...] = block_operator(tensor_ref, charges_ref, inner, group).astype(BF16)

    load_left.wait()
    load_initial(1).start()
    to, frm = iota((full, full), 0), iota((full, full), 1)
    keep_eye = jnp.where((to == frm) & (to < kept), 1.0, 0.0).astype(BF16)
    for i in range(CHUNKS):
        left_own[:, i * part : (i + 1) * part] = dot_t(keep_eye, raw[0, i * part : (i + 1) * part, :]).astype(BF16)

    def left_copy(i):
        span = pl.ds(i * (outer // LEFT_PARTS), outer // LEFT_PARTS)
        return pltpu.make_async_remote_copy(
            src_ref=left_own.at[span, :],
            dst_ref=left_in.at[span, :],
            send_sem=left_send.at[i],
            recv_sem=left_recv.at[i],
            device_id=(row, right_col),
            device_id_type=MESH,
        )

    pl.semaphore_wait(barrier, 1 + jnp.where(sends_any, 1, 0) + jnp.where(crosses, 1, 0) + jnp.where(relays, 1, 0))
    for i in range(LEFT_PARTS):
        left_copy(i).start()

    def boundary_copy(step, h, i):
        span = pl.ds(i * part, part)
        return pltpu.make_async_remote_copy(
            src_ref=outgoing.at[step, h, span, :],
            dst_ref=arrived.at[step, h, span, :],
            send_sem=send_sem.at[step, h, i],
            recv_sem=recv_sem.at[step, h, i],
            device_id=(row + 1, col),
            device_id_type=MESH,
        )

    def to_relay(step, i):
        span = pl.ds(i * part, part)
        return pltpu.make_async_remote_copy(
            src_ref=outgoing.at[step, 1, span, :],
            dst_ref=passing.at[step, span, :],
            send_sem=send_sem.at[step, 1, i],
            recv_sem=relay_recv.at[step, i],
            device_id=(opposite, far_col),
            device_id_type=MESH,
        )

    def from_relay(step, i):
        span = pl.ds(i * part, part)
        return pltpu.make_async_remote_copy(
            src_ref=passing.at[step, span, :],
            dst_ref=arrived.at[step, 1, span, :],
            send_sem=relay_send.at[step, i],
            recv_sem=recv_sem.at[step, 1, i],
            device_id=(lax.rem(row + turn_rows + 1, rows), far_col),
            device_id_type=MESH,
        )

    def pass_on(step, i):
        to_relay(step, i).wait_recv()
        from_relay(step, i).start()

    def relayed(step):
        shared = lax.rem(col, cols // 2) < 2
        main = (row == cross) | (row == rows - 1)
        return main | shared if step > 0 else main & shared

    def give(step, h, i):
        if h == 0:
            boundary_copy(step, 0, i).start()
        else:
            around = crosses & relayed(step)

            @pl.when(around)
            def _():
                to_relay(step, i).start()

            @pl.when(jnp.logical_not(around))
            def _():
                boundary_copy(step, 1, i).start()

    load_right.wait()
    split = jnp.where(frm == (to % keys) * inner + to // keys, 1.0, 0.0).astype(BF16)
    merge = jnp.where(frm == (to % inner) * keys + to // inner, 1.0, 0.0).astype(BF16)
    inside = frm < kept
    for i in range(CHUNKS):
        moved = dot(split, raw[1, i * part : (i + 1) * part, :])
        moved = jnp.where(inside, moved, 0.0).astype(BF16)
        for s in range(inner):
            for h in range(2):
                right_v[h, s // 2, i * keys : (i + 1) * keys, (s % 2) * lanes : (s % 2 + 1) * lanes] = moved[
                    s * keys : (s + 1) * keys, h * lanes : (h + 1) * lanes
                ]

    def absorb_sites(x, h, at):
        count = x.shape[0]
        for p in range(pairs):
            y = dot(x, right_v[h, p]).astype(BF16)
            half[h, 2 * p, :count] = y[:, :lanes]
            half[h, 2 * p + 1, :count] = y[:, lanes:]
        for g in range(0, count // block, 2):
            sides = [half[h, :, (g + n) * block : (g + n + 1) * block, :].reshape(full, lanes) for n in range(2)]
            y = dot(operator[...], jnp.concatenate(sides, axis=1)).astype(BF16)
            for d in range(inner):
                for n in range(2):
                    sites[h, d // 2, pl.ds(at + (g + n) * block, block), (d % 2) * lanes : (d % 2 + 1) * lanes] = y[
                        d * block : (d + 1) * block, n * lanes : (n + 1) * lanes
                    ]

    def merged(halves, i):
        span = pl.ds(i * keys, keys)
        sides = []
        for h in halves:
            stacked = [acc[h, d // 2, span, (d % 2) * lanes : (d % 2 + 1) * lanes] for d in range(inner)]
            sides.append(jnp.concatenate(stacked, axis=0).astype(BF16))
        return dot(merge, jnp.concatenate(sides, axis=1)).astype(BF16)

    flags = [jnp.where(start_ref[e] == row, 1.0, 0.0) for e in range(envs)]

    def choose(i, carry):
        load_initial(i).wait()

        at = pl.multiple_of(i * 4 * part, 4 * part)
        span = pl.ds(at, 4 * part)
        x = initial_v[0, span, :] * jnp.full((4 * part, outer), flags[0], F32).astype(BF16)
        for e in range(1, envs):
            x = x + initial_v[e, span, :] * jnp.full((4 * part, outer), flags[e], F32).astype(BF16)
        chosen[span, :] = x
        absorb_sites(x, 0, at)
        return carry

    lax.fori_loop(0, CHUNKS // 4, choose, 0)

    def give_first(h, lo=0, hi=CHUNKS):
        span = pl.ds(lo * keys, (hi - lo) * keys)
        for p in range(pairs):
            acc[h, p, span, :] = dot(left_in[span, :], sites[h, p])
        for i in range(lo, hi):
            outgoing[0, h, i * part : (i + 1) * part, :] = merged((h,), i)

            @pl.when(working(0))
            def _(i=i):
                give(0, h, i)

    def second(i, carry):
        at = pl.multiple_of(i * 4 * part, 4 * part)
        absorb_sites(chosen[pl.ds(at, 4 * part), :], 1, at)
        return carry

    late = lax.rem(col, cols // 2) == 0

    @pl.when(odd)
    def _():
        for i in range(LEFT_PARTS):
            left_copy(i).wait_recv()
        give_first(0)
        lax.fori_loop(0, CHUNKS // 4, second, 0)
        give_first(1)

    @pl.when(jnp.logical_not(odd))
    def _():
        lax.fori_loop(0, CHUNKS // 4, second, 0)

    @pl.when(jnp.logical_not(odd | late))
    def _():
        for i in range(LEFT_PARTS):
            left_copy(i).wait_recv()
        for h in range(2):
            give_first(h)

    @pl.when(late)
    def _():
        for n in range(2):
            for i in range(LEFT_PARTS // 2):
                left_copy(n * LEFT_PARTS // 2 + i).wait_recv()
            for h in range(2):
                give_first(h, n * CHUNKS // 2, (n + 1) * CHUNKS // 2)

    @pl.when(relays & relayed(0))
    def _():
        for i in range(CHUNKS):
            pass_on(0, i)

    @pl.when(relays & relayed(1))
    def _():
        for i in range(CHUNKS):
            pass_on(1, i)

    in_turn = jnp.logical_not(lands)

    def later(step):
        def take(i, carry, count=2, last=False):
            for n in range(count):
                for h in range(2):
                    boundary_copy(step - 1, h, i * count + n).wait_recv()

            if step < ABSORB - 1 and count == 2:
                @pl.when(in_turn & jnp.logical_not(odd) & (i == 1))
                def _():
                    pl.semaphore_signal(turn, inc=1, device_id=(row, right_col), device_id_type=MESH)

            at = pl.multiple_of(i * count * part, count * part)
            span = pl.ds(at, count * part)
            x = jnp.concatenate([arrived[step - 1, h, span, :] for h in range(2)], axis=1)
            for h in range(2):
                absorb_sites(x, h, at)
            for h in range(2):
                for p in range(pairs):
                    total = acc[h, p] + dot(left_in[:, span], sites[h, p, span, :])
                    if last:
                        for n in range(2):
                            out_ref[2 * p + n, :, h * lanes : (h + 1) * lanes] = total[:, n * lanes : (n + 1) * lanes].astype(BF16)
                    else:
                        acc[h, p] = total
            return carry

        acc[...] = jnp.zeros_like(acc)
        lax.fori_loop(0, CHUNKS // 2 - 1, take, 0)
        if step < ABSORB - 1:
            lax.fori_loop(CHUNKS - 2, CHUNKS, functools.partial(take, count=1), 0)
        else:
            take(CHUNKS // 2 - 1, 0, last=True)
            return

        @pl.when(in_turn & odd)
        def _():
            pl.semaphore_wait(turn, 1)

        for i in range(CHUNKS):
            made = merged((0, 1), i)
            for h in range(2):
                outgoing[step, h, i * part : (i + 1) * part, :] = made[:, h * lanes : (h + 1) * lanes]
                give(step, h, i)

    for step in range(1, ABSORB):

        @pl.when(working(step))
        def _(step=step):
            later(step)

    @pl.when(jnp.logical_not(working(ABSORB - 1)))
    def _():
        out_ref[...] = jnp.zeros_like(out_ref)

    for i in range(LEFT_PARTS):
        left_copy(i).wait_send()

    for step in range(ABSORB - 1):

        @pl.when(working(step))
        def _(step=step):
            for h in range(2):
                for i in range(CHUNKS):
                    boundary_copy(step, h, i).wait_send()

        @pl.when(relays & relayed(step))
        def _(step=step):
            for i in range(CHUNKS):
                from_relay(step, i).wait_send()


def shards(start_rows, initial, site_tensors, charges, right_proj, left_proj, kept_ranks):
    envs, _, outer, inner, _ = initial.shape
    size = outer * inner
    smem = pl.BlockSpec(memory_space=pltpu.SMEM)
    vmem = pl.BlockSpec(memory_space=pltpu.VMEM)
    hbm = pl.BlockSpec(memory_space=pltpu.HBM)
    out = pl.pallas_call(
        functools.partial(kernel, outer, inner, envs),
        out_shape=pltpu.VMEM((inner, outer, outer), BF16),
        in_specs=[smem, smem, smem, hbm, hbm, hbm, hbm],
        out_specs=vmem,
        scratch_shapes=[
            pltpu.VMEM((1, inner**4), BF16),
            pltpu.VMEM((envs, size, outer), BF16),
            pltpu.VMEM((size, outer), BF16),
            pltpu.VMEM((2, size, outer), BF16),
            pltpu.VMEM((2, inner // 2, outer, outer), BF16),
            pltpu.VMEM((outer, size), BF16),
            pltpu.VMEM((outer, size), BF16),
            pltpu.VMEM((2, inner, 4 * size // CHUNKS, outer // 2), BF16),
            pltpu.VMEM((2, inner // 2, size, outer), BF16),
            pltpu.VMEM((2, inner // 2, outer, outer), F32),
            pltpu.VMEM((outer, outer), BF16),
            pltpu.VMEM((ABSORB - 1, 2, size, outer // 2), BF16),
            pltpu.VMEM((ABSORB - 1, 2, size, outer // 2), BF16),
            pltpu.SemaphoreType.DMA((3,)),
            pltpu.SemaphoreType.DMA((CHUNKS // 4,)),
            pltpu.SemaphoreType.DMA((LEFT_PARTS,)),
            pltpu.SemaphoreType.DMA((LEFT_PARTS,)),
            pltpu.SemaphoreType.DMA((ABSORB - 1, 2, CHUNKS)),
            pltpu.SemaphoreType.DMA((ABSORB - 1, 2, CHUNKS)),
            pltpu.VMEM((ABSORB - 1, size, outer // 2), BF16),
            pltpu.SemaphoreType.DMA((ABSORB - 1, CHUNKS)),
            pltpu.SemaphoreType.DMA((ABSORB - 1, CHUNKS)),
            pltpu.SemaphoreType.REGULAR,
        ],
        compiler_params=pltpu.CompilerParams(
            collective_id=0, has_side_effects=True, vmem_limit_bytes=58 * 1024 * 1024
        ),
        cost_estimate=pl.CostEstimate(
            flops=ABSORB * 6 * size * size * outer, bytes_accessed=8 * size * outer * 2, transcendentals=0
        ),
    )(
        start_rows,
        kept_ranks,
        charges[0, 0],
        site_tensors[0],
        initial.reshape(envs, size, outer),
        right_proj.reshape(size, outer),
        left_proj.reshape(size, outer),
    )
    return out.transpose(1, 0, 2)[None, None]


def solution(mesh):
    return jax.shard_map(
        shards,
        mesh=mesh,
        in_specs=(
            P(),
            P(None, "col", None, None, None),
            P("row", "col", None),
            P("row", "col", None, None),
            P("row", "col", None, None, None),
            P("row", "col", None, None, None),
            P("row", "col"),
        ),
        out_specs=P("row", "col", None, None, None),
        check_vma=False,
    )
```
